32 devices in a mesh: lane: 4 (over y, x), section: 2 (over core), tp: 4 (over z).
Axes of the slice: x: 2, y: 2, z: 4, core: 2. Of those that a mesh axis runs over, the one named last changes fastest.
Arguments:
- merge_hidden: bfloat16 [2048, 5120], P('lane', 'section'), may hold values from -6 to 6
- merge_weight: bfloat16 [5120, 8192], P('section', 'tp'), may hold values from -0.25 to 0.25
- merge_bias: float32 [8192], P('tp'), may hold values from -3 to 3
- row_dest: int32 [2048], P(('lane', 'section')), may hold values from -1 to 3, as said below
- image_pos: int32 [4, 2, 4, 4], P('lane', 'section'), may hold values from -1 to 255, as said below
- text_embed: bfloat16 [2048, 8192], P(('lane', 'section'), 'tp'), may hold values from -8 to 8
- norm_gain: float32 [8192], P('tp'), may hold values from 0.25 to 1.75
- kv_weight: bfloat16 [8192, 2048], P('tp'), may hold values from -0.0625 to 0.0625
- kv_grad: bfloat16 [2048, 2048], P(('lane', 'section')), may hold values from -6 to 6
Outputs:
- key_value: bfloat16 [2048, 2048], P(('lane', 'section'), 'tp')
- embed_grad: bfloat16 [2048, 8192], P(('lane', 'section'), 'tp')
- image_grad: bfloat16 [2048, 8192], P(('lane', 'section'), 'tp')
The draws below stay inside these ranges and needn't reach their ends.
Inputs may be any that keep to these rules, and one draw needn't show every extreme that they name: `row_dest`: rows come in blocks of 256: block s of lane j is rows j * 512 + s * 256 onward. Rows of one block that go to one lane number at most 4; every block sends 4 rows to some lane, and for every s some lane receives 4 rows from block s of every lane. image_pos[l, s, j, k] is the position, among the 256 tokens of block s of lane l (tokens l * 512 + s * 256 onward), of the k-th row (in row order) that block s of lane j sends to lane l, and -1 where that block sends fewer than k + 1 rows to lane l; the positions taken in one block are distinct.
All inputs are finite; a program needn't handle non-finite values.
Results may differ from the reference program's by a relative error of at most 0.007.
Values may be sent and summed in bfloat16 or wider, within the bound.
No kernel may reach another device: no remote copies, remote signals or barrier semaphores. Data moves between devices by JAX's collectives and lax.ppermute only.
A program may use at most 64 MiB of HBM per device.

```python
import math
from functools import partial
import jax
import jax.numpy as jnp
from jax import lax

D = 8192
VD = 5120
TOK = 512
E_DEV = 512
CAP = 4
KV2 = 2048
TOK_BLOCK = 256
ROW_BLOCK = 256
TOKENS = 2048
ROWS = 2048


def section_tables(key):
    lane_count = ROWS // E_DEV
    key_counts, key_shift, key_full, key_order, key_place = jax.random.split(key, 5)
    counts = jax.random.randint(key_counts, (lane_count, lane_count), 0, CAP + 1)
    offset_lane = jax.random.randint(key_shift, (), 0, lane_count)
    source_ids = jnp.arange(lane_count)
    counts = counts.at[source_ids, (source_ids + offset_lane) % lane_count].set(CAP)
    full_lane = jax.random.randint(key_full, (), 0, lane_count)
    counts = counts.at[:, full_lane].set(CAP)
    orders = jax.vmap(partial(jax.random.permutation, x=lane_count))(jax.random.split(key_order, lane_count))
    ordered = jnp.take_along_axis(counts, orders, axis=1)
    row_ends = jnp.cumsum(ordered, axis=1)
    row_index = jnp.arange(ROW_BLOCK)
    group_index = jnp.sum(row_index[None, :, None] >= row_ends[:, None, :], axis=2)
    picked = jnp.take_along_axis(orders, jnp.minimum(group_index, lane_count - 1), axis=1)
    row_dest = jnp.where(group_index < lane_count, picked, -1).astype(jnp.int32)
    offsets = jnp.cumsum(counts, axis=0) - counts
    position_perms = jax.vmap(partial(jax.random.permutation, x=TOK_BLOCK))(jax.random.split(key_place, lane_count))
    slot_index = jnp.arange(CAP)
    flat_index = jnp.minimum(offsets.T[:, :, None] + slot_index[None, None, :], TOK_BLOCK - 1)
    gathered = jnp.take_along_axis(position_perms, flat_index.reshape(lane_count, -1), axis=1).reshape(lane_count, lane_count, CAP)
    is_valid = slot_index[None, None, :] < counts.T[:, :, None]
    image_pos = jnp.where(is_valid, gathered, -1).astype(jnp.int32)
    return (row_dest, image_pos)


def routing_tables(key):
    section_count = TOK // TOK_BLOCK
    base = jax.random.fold_in(key, 71)
    row_dest, image_pos = jax.vmap(section_tables)(jax.random.split(base, section_count))
    return (jnp.transpose(row_dest, (1, 0, 2)).reshape(-1), jnp.transpose(image_pos, (1, 0, 2, 3)))


def draw_row_dest(key, part):
    return routing_tables(key)[0]


def draw_image_pos(key, part):
    return routing_tables(key)[1]


def draw_text_embed(key, part):
    base = jax.random.fold_in(key, 13)
    key_normal, key_rough = jax.random.split(base, 2)
    column = jnp.arange(D, dtype=jnp.float32) / (D - 1)
    rough = jax.random.uniform(key_rough, (D,), minval=0.7, maxval=1.4)
    values = jax.random.normal(key_normal, (TOKENS, D)) * 0.6 * 3.0 ** column * rough
    return jnp.clip(values, -8.0, 8.0).astype(jnp.bfloat16)


def draw_merge_weight(key, part):
    base = jax.random.fold_in(key, 29)
    key_normal, key_rough = jax.random.split(base, 2)
    column = jnp.arange(D, dtype=jnp.float32) / (D - 1)
    rough = jax.random.uniform(key_rough, (D,), minval=0.7, maxval=1.4)
    values = jax.random.normal(key_normal, (VD, D)) * 0.6 * 3.0 ** column * rough
    return jnp.clip(values / math.sqrt(VD), -0.25, 0.25).astype(jnp.bfloat16)


def level_of(rng, dims, cuts, least, largest):
    level = 1.0
    for dim, shards_of in cuts:
        steps = jax.random.uniform(jax.random.fold_in(jax.random.fold_in(rng, 6), dim), (shards_of,), jnp.float32, least / len(cuts), largest / len(cuts))
        level = level * jnp.repeat(jnp.exp(steps), dims[dim] // shards_of).reshape((-1,) + (1,) * (len(dims) - 1 - dim))
    return level


def centred(stream_key, dims, spread, limit, cuts=(), held_as=jnp.bfloat16):
    result = spread * jax.random.normal(stream_key, dims, jnp.float32)
    if cuts:
        result = result * level_of(stream_key, dims, cuts, -0.22, 0.18)
    return jnp.clip(result, -limit, limit).astype(held_as)


def setup_inputs(seed: int = 0) -> dict:
    seeds = jax.random.split(jax.random.key(seed), 10)
    return {
        "merge_hidden": centred(seeds[0], (ROWS, VD), 1.0, 6.0, ((0, 4), (1, 2))),
        "merge_weight": draw_merge_weight(jax.random.fold_in(seeds[9], 71), 0),
        "merge_bias": centred(seeds[2], (D,), 0.5, 3.0, ((0, 4),), jnp.float32),
        "row_dest": draw_row_dest(jax.random.fold_in(seeds[9], 71), 0),
        "image_pos": draw_image_pos(jax.random.fold_in(seeds[9], 71), 0),
        "text_embed": draw_text_embed(jax.random.fold_in(seeds[9], 71), 0),
        "norm_gain": jnp.clip(1.0 + 0.15 * jax.random.normal(seeds[6], (D,), jnp.float32), 0.25, 1.75),
        "kv_weight": centred(seeds[7], (D, KV2), D ** -0.5, 0.0625, ((0, 4),)),
        "kv_grad": centred(seeds[8], (TOKENS, KV2), 1.0, 6.0, ((0, 8),)),
    }


EPSILON = 1e-06

def route_targets(row_dest, image_pos):
    lane_count = image_pos.shape[0]
    section_count = image_pos.shape[1]
    block_tokens = TOK // section_count
    per_block = row_dest.reshape(lane_count, section_count, -1)
    lane_ids = jnp.arange(lane_count, dtype=jnp.int32)
    matches = (per_block[:, :, :, None] == lane_ids[None, None, None, :]).astype(jnp.int32)
    before = jnp.cumsum(matches, axis=2) - matches
    row_rank = lax.optimization_barrier(jnp.sum(before * matches, axis=3)).astype(jnp.int32)
    is_valid = per_block >= 0
    dest_lane = jnp.where(is_valid, per_block, 0).astype(jnp.int32)
    source_lane = jnp.broadcast_to(lane_ids[:, None, None], per_block.shape)
    section_ids = jnp.broadcast_to(jnp.arange(section_count, dtype=jnp.int32)[None, :, None], per_block.shape)
    position = image_pos[dest_lane, section_ids, source_lane, jnp.clip(row_rank, 0, image_pos.shape[3] - 1)]
    target = (dest_lane * TOK + section_ids * block_tokens + position).astype(jnp.int32)
    return (is_valid.reshape(-1), target.reshape(-1))

def reference(merge_hidden, merge_weight, merge_bias, row_dest, image_pos, text_embed, norm_gain, kv_weight, kv_grad):
    activated = jax.nn.gelu(merge_hidden.astype(jnp.float32), approximate=False).astype(jnp.bfloat16)
    image_rows = (jnp.dot(activated, merge_weight, preferred_element_type=jnp.float32) + merge_bias).astype(jnp.bfloat16)
    is_valid, target = route_targets(row_dest, image_pos)
    target_row = jnp.where(is_valid, target, TOKENS).astype(jnp.int32)
    stream = text_embed.at[target_row].set(image_rows, mode='drop')
    lane_count = image_pos.shape[0]

    def per_lane(operands):
        lane_rows, lane_grad = operands
        widened = lane_rows.astype(jnp.float32)
        inv_rms = lax.rsqrt(lax.optimization_barrier(jnp.mean(widened * widened, axis=1, keepdims=True)) + EPSILON)
        normed = (widened * inv_rms * norm_gain).astype(jnp.bfloat16)
        key_value = jnp.dot(normed, kv_weight, preferred_element_type=jnp.float32).astype(jnp.bfloat16)
        normed_grad = jnp.dot(lane_grad, kv_weight.T, preferred_element_type=jnp.float32)
        row_dot = lax.optimization_barrier(jnp.sum(widened * norm_gain * normed_grad, axis=1, keepdims=True))
        embed_grad = (inv_rms * norm_gain * normed_grad - widened * inv_rms ** 3 * row_dot / D).astype(jnp.bfloat16)
        return (key_value, embed_grad)
    key_value, embed_grad = lax.map(per_lane, (stream.reshape(lane_count, TOK, D), kv_grad.reshape(lane_count, TOK, KV2)))
    key_value = key_value.reshape(TOKENS, KV2)
    embed_grad = embed_grad.reshape(TOKENS, D)
    picked = embed_grad[jnp.where(is_valid, target, 0).astype(jnp.int32)]
    image_grad = jnp.where(is_valid[:, None], picked, jnp.zeros_like(picked)).astype(jnp.bfloat16)
    return (key_value, embed_grad, image_grad)
```

```python
import math

import jax
import jax.numpy as jnp
import numpy as np
from jax import lax
from jax.experimental import pallas as pl
from jax.experimental.pallas import tpu as pltpu
from jax.sharding import PartitionSpec as P

EPSILON = 1e-06
F32 = jnp.float32
BF16 = jnp.bfloat16
MIB = 1 << 20
VMEM = pl.BlockSpec(memory_space=pltpu.VMEM)
ANY = pl.BlockSpec(memory_space=pl.ANY)
SMEM = pl.BlockSpec(memory_space=pltpu.SMEM)


def round_up(value, step):
    return -(-value // step) * step


def dot(a, b):
    return jnp.dot(a, b, preferred_element_type=F32)


def dot_dims(a, b, dim_a, dim_b):
    return lax.dot_general(a, b, (((dim_a,), (dim_b,)), ((), ())), preferred_element_type=F32)


def iota(shape, dim):
    return lax.broadcasted_iota(jnp.int32, shape, dim)


def one_hot(column, width):
    return (column == iota((column.shape[0], width), 1)).astype(F32).astype(BF16)


def text_kernel(tp_count, order_ref, text_hbm, gain_ref, grad_hbm, weight_hbm, *refs):
    parts = refs[:tp_count]
    weight, sums, text, grad, weight_sem, row_sem = refs[tp_count:]
    cols = weight.shape[1] // tp_count
    text_copy = pltpu.make_async_copy(text_hbm, text, row_sem.at[0])
    grad_copy = pltpu.make_async_copy(grad_hbm, grad, row_sem.at[1])
    text_copy.start()
    copies = []
    for k in range(tp_count):
        span = pl.ds(pl.multiple_of(order_ref[k] * cols, cols), cols)
        copy = pltpu.make_async_copy(weight_hbm.at[:, span], weight.at[:, span], weight_sem.at[k])
        copy.start()
        copies.append(copy)
        if k == 0:
            grad_copy.start()
    text_copy.wait()
    wide = text[...].astype(F32)
    squares = jnp.sum(wide * wide, axis=1, keepdims=True)
    scaled = (wide * gain_ref[...]).astype(BF16)
    dots = jnp.zeros_like(squares)
    grad_copy.wait()
    for k in range(tp_count):
        span = pl.ds(pl.multiple_of(order_ref[k] * cols, cols), cols)
        copies[k].wait()
        part = dot(scaled, weight[:, span])
        parts[k][...] = part.astype(parts[k].dtype)
        dots = dots + jnp.sum(part * grad[:, span].astype(F32), axis=1, keepdims=True)
    lane = iota((text.shape[0], 128), 1)
    sums[...] = jnp.where(lane == 0, squares, jnp.where(lane == 1, dots, 0.0)).T[:8]


def gather_kernel(group, cap, section_ref, own_ref, other_ref, pos_ref, slot_ref, hidden, grad, payload, send_table):
    rows = payload.shape[0]
    block = own_ref.shape[1]
    row_id = iota((rows, block), 0)
    shift = int(math.log2(group))
    lane_id = row_id >> shift
    place = row_id & (group - 1)
    earlier = (iota((block, block), 0) < iota((block, block), 1)).astype(F32).astype(BF16)

    def select(dest, first):
        match = dest == lane_id
        rank = dot(match.astype(F32).astype(BF16), earlier)
        return (match & (rank == (place - first).astype(F32))).astype(F32).astype(BF16)

    own = select(own_ref[...], 0)
    other = select(other_ref[...], cap)
    section = section_ref[0]
    own_rows = pl.ds(pl.multiple_of(section * block, block), block)
    other_rows = pl.ds(pl.multiple_of((1 - section) * block, block), block)
    picked = dot(own, hidden[own_rows, :]) + dot(other, hidden[other_rows, :])
    active = 0.5 * picked * (1.0 + lax.erf(picked * np.float32(math.sqrt(0.5))))
    grad_rows = dot(one_hot(pos_ref[...], block), grad[...])
    width = grad_rows.shape[1]
    payload[:, :width] = (active[:, :width] + grad_rows).astype(BF16)
    if width < payload.shape[1]:
        payload[:, width:] = active[:, width:].astype(BF16)
    send_table[...] = dot(one_hot(slot_ref[...], rows), own).astype(BF16)


def merge_kernel(cap, slot_ref, got, sent, weight, own, other, grad_rows):
    rows = got.shape[0]
    width = grad_rows.shape[1]
    slots = slot_ref.shape[0]
    first = one_hot(slot_ref[...], rows)
    second = one_hot(slot_ref[...] + cap, rows)
    third = one_hot(slot_ref[...] + 2 * cap, rows)
    picked = jnp.concatenate(
        [dot(first, got[...]), dot(first, sent[...]), dot(second, got[...]), dot(second, sent[...])], axis=0
    ).astype(BF16)
    grad_rows[:slots] = dot(third, sent[:, :width]).astype(BF16)
    grad_rows[slots:] = dot(third, got[:, :width]).astype(BF16)
    cols = weight.shape[1]
    step = min(512, cols)
    for c in range(0, cols, step):
        total = dot(picked, weight[:, c : c + step])
        own[:, c : c + step] = total[: 2 * slots]
        other[:, c : c + step] = total[2 * slots :].astype(BF16)


def slot_kernel(tp_count, sum_rows, own, other, bias, gain, weight, grad_rows, text_sums, rows, payload):
    slots2 = own.shape[0]
    slots = slots2 // 2
    placed = (own[...] + other[...].astype(F32) + bias[...]).astype(BF16)
    rows[...] = placed
    wide = placed.astype(F32)
    squares = jnp.sum(wide * wide, axis=1, keepdims=True)
    scaled = (wide * gain[...]).astype(BF16)
    cols = payload.shape[1]
    height = slots + sum_rows
    dots = jnp.zeros_like(squares)
    for d in range(tp_count):
        part = dot(scaled, weight[:, d * cols : (d + 1) * cols])
        dots = dots + jnp.sum(part * grad_rows[:, d * cols : (d + 1) * cols].astype(F32), axis=1, keepdims=True)
        payload[d * height : d * height + slots] = part[:slots].astype(BF16)
    lane = iota((slots2, 128), 1)
    columns = jnp.where(lane == 0, squares, jnp.where(lane == 1, dots, 0.0))
    padded = round_up(slots2, 128)
    if padded > slots2:
        columns = jnp.concatenate([columns, jnp.zeros((padded - slots2, 128), F32)], axis=0)
    turned = columns.T
    pieces = []
    for i in range(2):
        total = jnp.concatenate([text_sums[i : i + 1], turned[i : i + 1]], axis=1)
        high = total.astype(BF16).astype(F32)
        pieces += [high, total - high]
    line = jnp.concatenate(pieces, axis=1)
    message = jnp.zeros((sum_rows, cols), F32)
    sublane = iota((sum_rows, cols), 0)
    for i in range(line.shape[1] // cols):
        message = jnp.where(sublane == i, line[:, i * cols : (i + 1) * cols], message)
    message = message.astype(BF16)
    for d in range(tp_count):
        payload[d * height + slots : (d + 1) * height] = message


def grad_kernel(grad, grad_rows, weight, out):
    tokens = grad.shape[0]
    step = min(512, weight.shape[0])
    for c in range(0, weight.shape[0], step):
        piece = weight[c : c + step, :]
        out[:tokens, c : c + step] = dot_dims(grad[...], piece, 1, 1)
        out[tokens:, c : c + step] = dot_dims(grad_rows[...], piece, 1, 1)


def final_kernel(
    tp_count, features, got, rows, normed_grad, text, gain, place_table, send_table, embed_grad, image_grad, kv_rows, inv_out
):
    slots2 = rows.shape[0]
    slots = slots2 // 2
    tokens, cols = text.shape[0], got.shape[1]
    height = got.shape[0] // tp_count
    total = got[:height].astype(F32)
    for d in range(1, tp_count):
        total = total + got[d * height : (d + 1) * height].astype(F32)
    span = tokens + round_up(slots2, 128)
    line = jnp.concatenate([total[slots + i : slots + i + 1] for i in range(4 * span // cols)], axis=1)
    squares = line[:, :span] + line[:, span : 2 * span]
    dots = line[:, 2 * span : 3 * span] + line[:, 3 * span :]
    inv = lax.rsqrt(squares / features + EPSILON)
    slope = inv * inv * inv * dots / features
    sublane = iota((128, span), 0)
    turned = jnp.where(sublane == 0, inv, jnp.where(sublane == 1, slope, 0.0)).T
    inv_col, slope_col = turned[:, 0:1], turned[:, 1:2]
    inv_out[...] = jnp.broadcast_to(inv_col[:tokens], inv_out.shape)
    kv_rows[...] = (total[:slots] * inv_col[tokens : tokens + slots]).astype(BF16)
    is_image = jnp.sum(place_table[...].astype(F32), axis=1, keepdims=True) > 0.0
    step = min(512, text.shape[1])
    for c in range(0, text.shape[1], step):
        cut = slice(c, c + step)
        row_grad = (
            inv_col[tokens : tokens + slots2] * gain[:, cut] * normed_grad[tokens:, cut]
            - rows[:, cut].astype(F32) * slope_col[tokens : tokens + slots2]
        ).astype(BF16)
        token_grad = inv_col[:tokens] * gain[:, cut] * normed_grad[:tokens, cut] - text[:, cut].astype(F32) * slope_col[:tokens]
        embed_grad[:, cut] = jnp.where(is_image, dot(place_table[...], row_grad[:slots]), token_grad).astype(BF16)
        image_grad[:, cut] = dot_dims(send_table[...], row_grad[slots:], 0, 0).astype(BF16)


def key_value_kernel(count, *refs):
    parts, (inv, place_table, kv_rows, out) = refs[:count], refs[count:]
    total = parts[0][...].astype(F32)
    for part in parts[1:]:
        total = total + part[...].astype(F32)
    is_image = jnp.sum(place_table[...].astype(F32), axis=1, keepdims=True) > 0.0
    out[...] = jnp.where(is_image, dot(place_table[...], kv_rows[...]), total * inv[:, 0:1]).astype(BF16)


def params(mib):
    return pltpu.CompilerParams(vmem_limit_bytes=mib * MIB)


def shape(dims, dtype):
    return jax.ShapeDtypeStruct(dims, dtype)


def on_device(
    merge_hidden, merge_weight, merge_bias, row_dest, image_pos, text_embed, norm_gain, kv_weight, kv_grad
):
    lane_count, tp_count = lax.axis_size("lane"), lax.axis_size("tp")
    tp_id = lax.axis_index("tp")
    section_id = lax.axis_index("section")
    tokens, features = text_embed.shape
    kv_cols = kv_weight.shape[1]
    cols = kv_cols // tp_count
    cap = image_pos.shape[3]
    slots = lane_count * cap
    slots2 = 2 * slots
    group = max(16, 1 << (3 * cap - 1).bit_length())
    rows = lane_count * group
    width = max(merge_hidden.shape[1], kv_cols)
    block = row_dest.shape[0]
    gain = norm_gain.reshape(1, features)
    bias = merge_bias.reshape(1, features)

    own_dest = row_dest.reshape(1, block)
    other_dest = lax.ppermute(own_dest, "section", [(0, 1), (1, 0)])

    steps = sorted(range(tp_count), key=lambda k: -k)
    order = jnp.stack([tp_id ^ k for k in steps]).astype(jnp.int32)
    *parts, weight, text_sums = pl.pallas_call(
        lambda *refs: text_kernel(tp_count, *refs),
        out_shape=[shape((tokens, cols), F32 if k == 0 else BF16) for k in steps]
        + [pltpu.VMEM(kv_weight.shape, BF16), shape((8, tokens), F32)],
        in_specs=[SMEM, ANY, VMEM, ANY, ANY],
        out_specs=[VMEM] * (tp_count + 2),
        scratch_shapes=[
            pltpu.VMEM(text_embed.shape, BF16),
            pltpu.VMEM(kv_grad.shape, BF16),
            pltpu.SemaphoreType.DMA((tp_count,)),
            pltpu.SemaphoreType.DMA((2,)),
        ],
        compiler_params=params(24),
        name="text_kv",
    )(order, text_embed, gain, kv_grad, kv_weight)
    arrived = [parts[-1]]
    for k, part in zip(steps[:-1], parts[:-1]):
        arrived.append(lax.ppermute(part, "tp", [(i, i ^ k) for i in range(tp_count)]))

    slot_rows = np.arange(slots, dtype=np.int32)
    slot_rows = jnp.asarray((slot_rows // cap * group + slot_rows % cap)[:, None])
    positions = image_pos.reshape(lane_count, cap)
    pos_column = jnp.pad(positions, ((0, 0), (2 * cap, group - 3 * cap)), constant_values=-1).reshape(rows, 1)
    place_table = (positions.reshape(1, slots) == jnp.arange(tokens, dtype=jnp.int32)[:, None]).astype(BF16)
    sent, send_table = pl.pallas_call(
        lambda *refs: gather_kernel(group, cap, *refs),
        out_shape=[shape((rows, width), BF16), shape((slots, block), BF16)],
        in_specs=[SMEM] + [VMEM] * 6,
        out_specs=[VMEM] * 2,
        compiler_params=params(24),
        name="gather_rows",
    )(section_id.astype(jnp.int32).reshape(1), own_dest, other_dest, pos_column, slot_rows, merge_hidden, kv_grad)
    got = lax.all_to_all(sent, "lane", 0, 0, tiled=True)

    own, other, grad_rows = pl.pallas_call(
        lambda *refs: merge_kernel(cap, *refs),
        out_shape=[shape((slots2, features), F32), shape((slots2, features), BF16), shape((slots2, kv_cols), BF16)],
        in_specs=[VMEM] * 4,
        out_specs=[VMEM] * 3,
        compiler_params=params(32),
        name="merge_rows",
    )(slot_rows, got, sent, merge_weight)
    other = lax.ppermute(other, "section", [(0, 1), (1, 0)])

    span = tokens + round_up(slots2, 128)
    sum_rows = round_up(-(-4 * span // cols), 16)
    placed, message = pl.pallas_call(
        lambda *refs: slot_kernel(tp_count, sum_rows, *refs),
        out_shape=[shape((slots2, features), BF16), shape((tp_count * (slots + sum_rows), cols), BF16)],
        in_specs=[VMEM] * 7,
        out_specs=[VMEM] * 2,
        compiler_params=params(24),
        name="slot_kv",
    )(own, other, bias, gain, weight, grad_rows, text_sums)
    messages = lax.all_to_all(message, "tp", 0, 0, tiled=True)

    normed_grad = pl.pallas_call(
        grad_kernel,
        out_shape=shape((tokens + slots2, features), F32),
        in_specs=[VMEM] * 3,
        out_specs=VMEM,
        compiler_params=params(24),
        name="normed_grad",
    )(kv_grad, grad_rows, weight)

    embed_grad, image_grad, kv_rows, inv = pl.pallas_call(
        lambda *refs: final_kernel(tp_count, features * tp_count, *refs),
        out_shape=[
            shape((tokens, features), BF16),
            shape((block, features), BF16),
            shape((slots, cols), BF16),
            shape((tokens, 128), F32),
        ],
        in_specs=[VMEM] * 7,
        out_specs=[VMEM] * 4,
        compiler_params=params(24),
        name="input_grads",
    )(messages, placed, normed_grad, text_embed, gain, place_table, send_table)

    key_value = pl.pallas_call(
        lambda *refs: key_value_kernel(tp_count, *refs),
        out_shape=shape((tokens, cols), BF16),
        in_specs=[VMEM] * (tp_count + 3),
        out_specs=VMEM,
        compiler_params=params(16),
        name="key_value",
    )(*arrived, inv, place_table, kv_rows)
    return (key_value, embed_grad, image_grad)


def solution(mesh):
    in_specs = (
        P("lane", "section"),
        P("section", "tp"),
        P("tp"),
        P(("lane", "section")),
        P("lane", "section", None, None),
        P(("lane", "section"), "tp"),
        P("tp"),
        P("tp", None),
        P(("lane", "section"), None),
    )
    out_specs = (
        P(("lane", "section"), "tp"),
        P(("lane", "section"), "tp"),
        P(("lane", "section"), "tp"),
    )
    return jax.shard_map(
        on_device, mesh=mesh, in_specs=in_specs, out_specs=out_specs, check_vma=False
    )
```

```python
import math

import jax
import jax.numpy as jnp
import numpy as np
from jax import lax
from jax.experimental import pallas as pl
from jax.experimental.pallas import tpu as pltpu
from jax.sharding import PartitionSpec as P

EPSILON = 1e-06
F32 = jnp.float32
BF16 = jnp.bfloat16
MIB = 1 << 20
VMEM = pl.BlockSpec(memory_space=pltpu.VMEM)
ANY = pl.BlockSpec(memory_space=pl.ANY)


def round_up(value, step):
    return -(-value // step) * step


def dot(a, b):
    return jnp.dot(a, b, preferred_element_type=F32)


def dot_dims(a, b, dim_a, dim_b):
    return lax.dot_general(a, b, (((dim_a,), (dim_b,)), ((), ())), preferred_element_type=F32)


def iota(shape, dim):
    return lax.broadcasted_iota(jnp.int32, shape, dim)


def one_hot(column, width):
    return (column == iota((column.shape[0], width), 1)).astype(F32).astype(BF16)


def peer_columns(axis, k, cols):
    return pl.ds(pl.multiple_of((lax.axis_index(axis) ^ k) * cols, cols), cols)


def picker(slots, rows, group, cap, first):
    row = iota((slots, rows), 1)
    place = (row & (group - 1)) - first
    slot = (row >> int(math.log2(group))) * cap + place
    return ((slot == iota((slots, rows), 0)) & (place >= 0) & (place < cap)).astype(F32).astype(BF16)


def mask(match):
    return match.astype(F32).astype(BF16)


def first_text_kernel(step, *refs):
    sources, (part, scaled, sums), kept, (gain, weight, sem) = refs[:7], refs[7:10], refs[10:15], refs[15:]
    text, grad = kept[:2]
    span = peer_columns("tp", step, part.shape[1])
    text_hbm, grad_hbm, dest_hbm, pos_hbm, hidden_hbm, gain_hbm, weight_hbm = sources
    pairs = [
        (text_hbm, text),
        (gain_hbm, gain),
        (weight_hbm.at[:, span], weight),
        (grad_hbm, grad),
        (dest_hbm, kept[2]),
        (pos_hbm, kept[3]),
        (hidden_hbm, kept[4]),
    ]
    copies = [pltpu.make_async_copy(source, target, sem.at[i]) for i, (source, target) in enumerate(pairs)]
    for copy in copies:
        copy.start()
    copies[0].wait()
    copies[1].wait()
    wide = text[...].astype(F32)
    squares = jnp.sum(wide * wide, axis=1, keepdims=True)
    scaled[...] = (wide * gain[...]).astype(BF16)
    copies[2].wait()
    product = dot(scaled[...], weight[...])
    part[...] = product.astype(BF16)
    copies[3].wait()
    dots = jnp.sum(product * grad[:, span].astype(F32), axis=1, keepdims=True)
    lane = iota(sums.shape, 1)
    sums[...] = jnp.where(lane == 0, squares, jnp.where(lane == 1, dots, 0.0))
    for copy in copies[4:]:
        copy.wait()


def text_kernel(steps, scaled, weight, grad, sums, *refs):
    parts, sums_out = refs[:-1], refs[-1]
    dots = jnp.zeros((scaled.shape[0], 1), F32)
    for step, part in zip(steps, parts):
        span = peer_columns("tp", step, part.shape[1])
        product = dot(scaled[...], weight[:, span])
        part[...] = product.astype(part.dtype)
        dots = dots + jnp.sum(product * grad[:, span].astype(F32), axis=1, keepdims=True)
    lane = iota(sums.shape, 1)
    sums_out[...] = (sums[...] + jnp.where(lane == 1, dots, 0.0)).T[:8]


def gather_kernel(lane_count, group, cap, own_ref, other_ref, pos_ref, hidden, grad, *refs):
    payloads, (send_table, place_table) = refs[:lane_count], refs[lane_count:]
    rows = lane_count * group
    slots = lane_count * cap
    block, tokens = own_ref.shape[1], grad.shape[0]
    lane = lax.axis_index("lane")
    row_id = iota((rows, block), 0)
    lane_id = (row_id >> int(math.log2(group))) ^ lane
    place = row_id & (group - 1)
    entry = place & (2 * cap - 1)
    earlier = mask(iota((block, block), 0) < iota((block, block), 1))

    def select(dest, first):
        match = dest == lane_id
        rank = dot(mask(match), earlier)
        return match & (rank == (entry - first).astype(F32))

    own = select(own_ref[...], 0)
    other = select(other_ref[...], cap)
    section = lax.axis_index("section")
    own_rows = pl.ds(pl.multiple_of(section * block, block), block)
    other_rows = pl.ds(pl.multiple_of((1 - section) * block, block), block)
    folds = group // (2 * cap)
    width = hidden.shape[1] // folds
    picked = jnp.zeros((rows, width), F32)
    for i in range(folds):
        here = (place >= 2 * cap * i) & (place < 2 * cap * (i + 1))
        cut = slice(i * width, (i + 1) * width)
        picked = picked + dot(mask(own & here), hidden[own_rows, cut]) + dot(mask(other & here), hidden[other_rows, cut])
    active = 0.5 * picked * (1.0 + lax.erf(picked * np.float32(math.sqrt(0.5))))

    lane_pick = mask((iota((rows, lane_count), 0) >> int(math.log2(group))) ^ lane == iota((rows, lane_count), 1))
    high, low = pos_ref[...] >> 7, pos_ref[...] & 127
    spread = dot(lane_pick, high.astype(F32).astype(BF16)) * 128.0 + dot(lane_pick, low.astype(F32).astype(BF16))
    chosen = (iota((rows, cap), 0) & (cap - 1)) == iota((rows, cap), 1)
    row_pos = jnp.sum(jnp.where(chosen, spread, 0.0), axis=1, keepdims=True)
    taken = row_pos == iota((rows, tokens), 1).astype(F32)
    taken_place = iota((rows, tokens), 0) & (group - 1)
    grad_folds = group // cap
    grad_width = grad.shape[1] // grad_folds
    grad_rows = jnp.zeros((rows, grad_width), F32)
    for i in range(grad_folds):
        here = (taken_place >= cap * i) & (taken_place < cap * (i + 1))
        grad_rows = grad_rows + dot(mask(taken & here), grad[:, i * grad_width : (i + 1) * grad_width])
    for k in range(lane_count):
        cut = slice(k * group, (k + 1) * group)
        payloads[k][:, :width] = active[cut].astype(BF16)
        payloads[k][:, width:] = grad_rows[cut].astype(BF16)
    first = picker(slots, rows, group, cap, 0)
    send_table[...] = dot(first, mask(own)).astype(BF16)
    place_table[...] = dot(first, mask(taken)).astype(BF16)


def merge_kernel(lane_count, cap, *refs):
    got_refs, sent_refs = (refs[0],) + refs[lane_count : 2 * lane_count - 1], refs[:lane_count]
    weight, text_part, first_part, own, other, grad_rows, text_total = refs[2 * lane_count - 1 :]
    text_total[...] = text_part[...] + first_part[...].astype(F32)
    group = refs[0].shape[0]
    rows = lane_count * group
    slots = lane_count * cap
    grad_width = grad_rows.shape[1] // (group // cap)
    width = refs[0].shape[1] - grad_width
    got = jnp.concatenate([ref[...] for ref in got_refs], axis=0)
    sent = jnp.concatenate([ref[...] for ref in sent_refs], axis=0)

    def unfold(table, first, step, cols):
        pieces = [dot(picker(slots, rows, group, cap, i), table[:, cols]) for i in range(first, group, step)]
        return jnp.concatenate(pieces, axis=1).astype(BF16)

    merged = slice(0, width)
    picked = jnp.concatenate(
        [unfold(table, first, 2 * cap, merged) for first in (0, cap) for table in (got, sent)], axis=0
    )
    grad_rows[:slots] = unfold(sent, 0, cap, slice(width, width + grad_width))
    grad_rows[slots:] = unfold(got, 0, cap, slice(width, width + grad_width))
    cols = weight.shape[1]
    step = min(512, cols)
    for c in range(0, cols, step):
        total = dot(picked, weight[:, c : c + step])
        own[:, c : c + step] = total[: 2 * slots]
        other[:, c : c + step] = total[2 * slots :].astype(BF16)


def slot_kernel(tp_count, sum_rows, own, other, bias, gain, weight, grad_rows, text_sums, rows, *messages):
    slots2 = own.shape[0]
    slots = slots2 // 2
    placed = (own[...] + other[...].astype(F32) + bias[...]).astype(BF16)
    rows[...] = placed
    wide = placed.astype(F32)
    squares = jnp.sum(wide * wide, axis=1, keepdims=True)
    scaled = (wide * gain[...]).astype(BF16)
    cols = messages[0].shape[1]
    dots = jnp.zeros_like(squares)
    for k in range(tp_count):
        span = peer_columns("tp", k, cols)
        part = dot(scaled, weight[:, span])
        dots = dots + jnp.sum(part * grad_rows[:, span].astype(F32), axis=1, keepdims=True)
        messages[k][:slots] = part[:slots].astype(BF16)
    lane = iota((slots2, 128), 1)
    columns = jnp.where(lane == 0, squares, jnp.where(lane == 1, dots, 0.0))
    padded = round_up(slots2, 128)
    if padded > slots2:
        columns = jnp.concatenate([columns, jnp.zeros((padded - slots2, 128), F32)], axis=0)
    turned = columns.T
    pieces = []
    for i in range(2):
        total = jnp.concatenate([text_sums[i : i + 1], turned[i : i + 1]], axis=1)
        high = total.astype(BF16).astype(F32)
        pieces += [high, total - high]
    line = jnp.concatenate(pieces, axis=1)
    message = jnp.zeros((sum_rows, cols), F32)
    sublane = iota((sum_rows, cols), 0)
    for i in range(line.shape[1] // cols):
        message = jnp.where(sublane == i, line[:, i * cols : (i + 1) * cols], message)
    for k in range(tp_count):
        messages[k][slots:] = message.astype(BF16)


def grad_kernel(grad, grad_rows, weight, gain, text, rows, place_table, out, stream):
    slots = grad_rows.shape[0] // 2
    joined = jnp.concatenate([grad[...], grad_rows[slots:]], axis=0)
    taken = dot_dims(place_table[...], jnp.ones((slots, 128), BF16), 0, 0)[:, 0:1] > 0.0
    step = min(512, weight.shape[0])
    for c in range(0, weight.shape[0], step):
        cut = slice(c, c + step)
        out[:, cut] = gain[:, cut] * dot_dims(joined, weight[cut, :], 1, 1)
        placed = dot_dims(place_table[...], rows[:slots, cut], 0, 0)
        stream[:, cut] = jnp.where(taken, placed, text[:, cut].astype(F32)).astype(BF16)


def final_kernel(tp_count, arrived_count, features, rows, scaled_grad, stream, place_table, send_table, *refs):
    messages, parts = refs[:tp_count], refs[tp_count : tp_count + arrived_count]
    key_value, embed_grad, image_grad, kv_buffer, embed_buffer, image_buffer, sem = refs[tp_count + arrived_count :]
    slots2 = rows.shape[0]
    slots = slots2 // 2
    tokens, cols = kv_buffer.shape
    total = messages[0][...].astype(F32)
    for message in messages[1:]:
        total = total + message[...].astype(F32)
    span = tokens + round_up(slots2, 128)
    line = jnp.concatenate([total[slots + i : slots + i + 1] for i in range(4 * span // cols)], axis=1)
    squares = line[:, :span] + line[:, span : 2 * span]
    dots = line[:, 2 * span : 3 * span] + line[:, 3 * span :]
    inv = lax.rsqrt(squares / features + EPSILON)
    slope = inv * inv * inv * dots / features
    sublane = iota((128, span), 0)
    turned = jnp.where(sublane == 0, inv, jnp.where(sublane == 1, slope, 0.0)).T
    slot_inv, slot_slope = turned[tokens : tokens + slots2, 0:1], turned[tokens : tokens + slots2, 1:2]
    table = place_table[...].astype(F32)
    taken = jnp.sum(table, axis=0, keepdims=True) > 0.0
    token_inv = jnp.where(taken, jnp.sum(table * slot_inv[:slots], axis=0, keepdims=True), inv[:, :tokens])
    token_slope = jnp.where(taken, jnp.sum(table * slot_slope[:slots], axis=0, keepdims=True), slope[:, :tokens])
    sublane = iota((128, tokens), 0)
    lines = jnp.where(sublane == 0, token_inv, jnp.where(sublane == 1, token_slope, 0.0))
    turned = jnp.where(sublane == 2, taken.astype(F32), lines).T
    inv_col, slope_col, taken_col = turned[:, 0:1], turned[:, 1:2], turned[:, 2:3] > 0.0

    copies = []

    def send(source, target):
        copy = pltpu.make_async_copy(source, target, sem.at[len(copies)])
        copy.start()
        copies.append(copy)

    step = stream.shape[1] // 2
    for c in range(0, stream.shape[1], step):
        cut = slice(c, c + step)
        embed_buffer[:, cut] = (inv_col * scaled_grad[:tokens, cut] - stream[:, cut].astype(F32) * slope_col).astype(BF16)
        send(embed_buffer.at[:, cut], embed_grad.at[:, cut])
        row_grad = slot_inv[slots:] * scaled_grad[tokens:, cut] - rows[slots:, cut].astype(F32) * slot_slope[slots:]
        image_buffer[:, cut] = dot_dims(send_table[...], row_grad.astype(BF16), 0, 0).astype(BF16)
        send(image_buffer.at[:, cut], image_grad.at[:, cut])
    kv_rows = (total[:slots] * slot_inv[:slots]).astype(BF16)
    kv_total = parts[0][...]
    for part in parts[1:]:
        kv_total = kv_total + part[...].astype(F32)
    kv_buffer[...] = jnp.where(taken_col, dot_dims(place_table[...], kv_rows, 0, 0), kv_total * inv_col).astype(BF16)
    send(kv_buffer, key_value)
    for copy in copies:
        copy.wait()


def params(mib=16):
    return pltpu.CompilerParams(vmem_limit_bytes=mib * MIB)


COST = pl.CostEstimate(flops=1024, bytes_accessed=1024, transcendentals=0)


def shape(dims, dtype):
    return jax.ShapeDtypeStruct(dims, dtype)


def call(kernel, name, operands, in_specs, outs, out_specs=None, scratch=(), cost=COST):
    return pl.pallas_call(
        kernel,
        out_shape=outs,
        in_specs=in_specs,
        out_specs=out_specs or [VMEM] * len(outs),
        scratch_shapes=scratch,
        compiler_params=params(),
        cost_estimate=cost,
        name=name,
    )(*operands)


def in_hbm(array):
    return pltpu.with_memory_space_constraint(array, pltpu.HBM)


def swap(array, axis, k):
    return lax.ppermute(array, axis, [(i, i ^ k) for i in range(lax.axis_size(axis))])


def on_device(
    merge_hidden, merge_weight, merge_bias, row_dest, image_pos, text_embed, norm_gain, kv_weight, kv_grad
):
    lane_count, tp_count = lax.axis_size("lane"), lax.axis_size("tp")
    tokens, features = text_embed.shape
    kv_cols = kv_weight.shape[1]
    cols = kv_cols // tp_count
    cap = image_pos.shape[3]
    slots = lane_count * cap
    slots2 = 2 * slots
    group = max(16, 2 * cap)
    width = merge_hidden.shape[1] // (group // (2 * cap)) + kv_cols // (group // cap)
    block = row_dest.shape[0]
    gain = norm_gain.reshape(1, features)
    bias = merge_bias.reshape(1, features)
    own_dest = row_dest.reshape(1, block)
    positions = image_pos.reshape(lane_count, cap)

    other_dest = swap(own_dest, "section", 1)
    half = tp_count // 2
    kept = (text_embed, kv_grad, own_dest, positions, merge_hidden)
    first_part, scaled, first_sums, text, grad, own_dest, positions, hidden = call(
        lambda *refs: first_text_kernel(half, *refs),
        "first_text_kv",
        [in_hbm(array) for array in kept + (gain, kv_weight)],
        [ANY] * 7,
        [shape((tokens, cols), BF16), shape((tokens, features), BF16), shape((tokens, 128), F32)]
        + [pltpu.VMEM(array.shape, array.dtype) for array in kept],
        scratch=[
            pltpu.VMEM((1, features), F32),
            pltpu.VMEM((features, cols), BF16),
            pltpu.SemaphoreType.DMA((7,)),
        ],
    )
    first_part, other_dest = lax.optimization_barrier((first_part, other_dest))
    first_part = swap(first_part, "tp", half)

    *sent, send_table, place_table = call(
        lambda *refs: gather_kernel(lane_count, group, cap, *refs),
        "gather_rows",
        [own_dest, other_dest, positions, hidden, grad],
        [VMEM] * 5,
        [shape((group, width), BF16)] * lane_count + [shape((slots, block), BF16), shape((slots, tokens), BF16)],
    )
    got = [swap(sent[k], "lane", k) for k in range(1, lane_count)]

    steps = [k for k in range(1, tp_count) if k != half] + [0]
    *parts, text_sums = call(
        lambda *refs: text_kernel(steps, *refs),
        "text_kv",
        [scaled, kv_weight, grad, first_sums],
        [VMEM] * 4,
        [shape((tokens, cols), BF16)] * (tp_count - 2) + [shape((tokens, cols), F32), shape((8, tokens), F32)],
    )
    arrived = [swap(part, "tp", k) for part, k in zip(parts, steps[:-1])]

    own, other, grad_rows, text_total = call(
        lambda *refs: merge_kernel(lane_count, cap, *refs),
        "merge_rows",
        [*sent, *got, merge_weight, parts[-1], first_part],
        [VMEM] * (2 * lane_count + 2),
        [
            shape((slots2, features), F32),
            shape((slots2, features), BF16),
            shape((slots2, kv_cols), BF16),
            shape((tokens, cols), F32),
        ],
    )
    other = swap(other, "section", 1)

    span = tokens + round_up(slots2, 128)
    sum_rows = round_up(-(-4 * span // cols), 16)
    placed, *messages = call(
        lambda *refs: slot_kernel(tp_count, sum_rows, *refs),
        "slot_kv",
        [own, other, bias, gain, kv_weight, grad_rows, text_sums],
        [VMEM] * 7,
        [shape((slots2, features), BF16)] + [shape((slots + sum_rows, cols), BF16)] * tp_count,
    )
    messages = [messages[0]] + [swap(messages[k], "tp", k) for k in range(1, tp_count)]

    scaled_grad, stream = call(
        grad_kernel,
        "normed_grad",
        [grad, grad_rows, kv_weight, gain, text, placed, place_table],
        [VMEM] * 7,
        [shape((tokens + slots, features), F32), shape((tokens, features), BF16)],
    )

    key_value, embed_grad, image_grad = call(
        lambda *refs: final_kernel(tp_count, tp_count - 1, features * tp_count, *refs),
        "outputs",
        [placed, scaled_grad, stream, place_table, send_table, *messages, text_total, *arrived],
        [VMEM] * (4 + 2 * tp_count),
        [shape((tokens, cols), BF16), shape((tokens, features), BF16), shape((block, features), BF16)],
        out_specs=[ANY] * 3,
        scratch=[
            pltpu.VMEM((tokens, cols), BF16),
            pltpu.VMEM((tokens, features), BF16),
            pltpu.VMEM((block, features), BF16),
            pltpu.SemaphoreType.DMA((5,)),
        ],
    )
    return (key_value, embed_grad, image_grad)


def solution(mesh):
    in_specs = (
        P("lane", "section"),
        P("section", "tp"),
        P("tp"),
        P(("lane", "section")),
        P("lane", "section", None, None),
        P(("lane", "section"), "tp"),
        P("tp"),
        P("tp", None),
        P(("lane", "section"), None),
    )
    out_specs = (
        P(("lane", "section"), "tp"),
        P(("lane", "section"), "tp"),
        P(("lane", "section"), "tp"),
    )
    return jax.shard_map(
        on_device, mesh=mesh, in_specs=in_specs, out_specs=out_specs, check_vma=False
    )
```

```python
import math

import jax
import jax.numpy as jnp
import numpy as np
from jax import lax
from jax.experimental import pallas as pl
from jax.experimental.pallas import tpu as pltpu
from jax.sharding import PartitionSpec as P

EPSILON = 1e-06
F32 = jnp.float32
BF16 = jnp.bfloat16
MIB = 1 << 20
VMEM = pl.BlockSpec(memory_space=pltpu.VMEM)
ANY = pl.BlockSpec(memory_space=pl.ANY)


def round_up(value, step):
    return -(-value // step) * step


def dot(a, b):
    return jnp.dot(a, b, preferred_element_type=F32)


def dot_dims(a, b, dim_a, dim_b):
    return lax.dot_general(a, b, (((dim_a,), (dim_b,)), ((), ())), preferred_element_type=F32)


def iota(shape, dim):
    return lax.broadcasted_iota(jnp.int32, shape, dim)


def one_hot(column, width):
    return (column == iota((column.shape[0], width), 1)).astype(F32).astype(BF16)


def peer_columns(axis, k, cols):
    return pl.ds(pl.multiple_of((lax.axis_index(axis) ^ k) * cols, cols), cols)


def picker(slots, rows, group, cap, first):
    row = iota((slots, rows), 1)
    place = (row & (group - 1)) - first
    slot = (row >> int(math.log2(group))) * cap + place
    return ((slot == iota((slots, rows), 0)) & (place >= 0) & (place < cap)).astype(F32).astype(BF16)


def mask(match):
    return match.astype(F32).astype(BF16)


def first_text_kernel(step, text_hbm, gain_hbm, weight_hbm, part, scaled, text, gain, weight, sem):
    span = peer_columns("tp", step, part.shape[1])
    gain_copy = pltpu.make_async_copy(gain_hbm, gain, sem.at[0])
    gain_copy.start()
    count = 4 if text.shape[1] % 512 == 0 else 1
    size = text.shape[1] // count
    cuts = [slice(i * size, (i + 1) * size) for i in range(count)]
    copies = []
    for i, cut in enumerate(cuts):
        pair = (
            pltpu.make_async_copy(text_hbm.at[:, cut], text.at[:, cut], sem.at[2 * i + 1]),
            pltpu.make_async_copy(weight_hbm.at[cut, span], weight.at[cut], sem.at[2 * i + 2]),
        )
        for copy in pair:
            copy.start()
        copies.append(pair)
    gain_copy.wait()
    total = jnp.zeros(part.shape, F32)
    for cut, pair in zip(cuts, copies):
        pair[0].wait()
        scaled[:, cut] = (text[:, cut].astype(F32) * gain[:, cut]).astype(BF16)
        pair[1].wait()
        total = total + dot(scaled[:, cut], weight[cut])
    part[...] = total.astype(BF16)


def text_kernel(first_step, steps, scaled, weight, grad, text, first_part, *refs):
    parts, sums = refs[:-1], refs[-1]
    cols = parts[0].shape[1]

    def row_dots(product, span):
        return jnp.sum(product * grad[:, span].astype(F32), axis=1, keepdims=True)

    dots = row_dots(first_part[...].astype(F32), peer_columns("tp", first_step, cols))
    for step, part in zip(steps, parts):
        span = peer_columns("tp", step, cols)
        product = dot(scaled[...], weight[:, span])
        part[...] = product.astype(part.dtype)
        dots = dots + row_dots(product, span)
    wide = text[...].astype(F32)
    squares = jnp.sum(wide * wide, axis=1, keepdims=True)
    lane = iota((text.shape[0], 128), 1)
    sums[...] = jnp.where(lane == 0, squares, jnp.where(lane == 1, dots, 0.0)).T[:8]


def gather_kernel(lane_count, group, cap, other_ref, own_hbm, pos_hbm, grad, hidden, *refs):
    payloads, (send_table, place_table, own_ref, pos_ref, sem) = refs[:lane_count], refs[lane_count:]
    pairs = [(own_hbm, own_ref), (pos_hbm, pos_ref)]
    copies = [pltpu.make_async_copy(source, target, sem.at[i]) for i, (source, target) in enumerate(pairs)]
    for copy in copies:
        copy.start()
    copies[0].wait()
    copies[1].wait()
    rows = lane_count * group
    slots = lane_count * cap
    block, tokens = own_ref.shape[1], grad.shape[0]
    lane = lax.axis_index("lane")
    row_id = iota((rows, block), 0)
    lane_id = (row_id >> int(math.log2(group))) ^ lane
    place = row_id & (group - 1)
    entry = place & (2 * cap - 1)
    earlier = mask(iota((block, block), 0) < iota((block, block), 1))

    def select(dest, first):
        match = dest == lane_id
        rank = dot(mask(match), earlier)
        return match & (rank == (entry - first).astype(F32))

    own = select(own_ref[...], 0)
    other = select(other_ref[...], cap)
    lane_pick = mask((iota((rows, lane_count), 0) >> int(math.log2(group))) ^ lane == iota((rows, lane_count), 1))
    high, low = pos_ref[...] >> 7, pos_ref[...] & 127
    spread = dot(lane_pick, high.astype(F32).astype(BF16)) * 128.0 + dot(lane_pick, low.astype(F32).astype(BF16))
    chosen = (iota((rows, cap), 0) & (cap - 1)) == iota((rows, cap), 1)
    row_pos = jnp.sum(jnp.where(chosen, spread, 0.0), axis=1, keepdims=True)
    taken = row_pos == iota((rows, tokens), 1).astype(F32)
    taken_place = iota((rows, tokens), 0) & (group - 1)
    grad_folds = group // cap
    grad_width = grad.shape[1] // grad_folds
    grad_rows = jnp.zeros((rows, grad_width), F32)
    for i in range(grad_folds):
        here = (taken_place >= cap * i) & (taken_place < cap * (i + 1))
        grad_rows = grad_rows + dot(mask(taken & here), grad[:, i * grad_width : (i + 1) * grad_width])
    section = lax.axis_index("section")
    own_rows = pl.ds(pl.multiple_of(section * block, block), block)
    other_rows = pl.ds(pl.multiple_of((1 - section) * block, block), block)
    folds = group // (2 * cap)
    width = hidden.shape[1] // folds
    picked = jnp.zeros((rows, width), F32)
    for i in range(folds):
        here = (place >= 2 * cap * i) & (place < 2 * cap * (i + 1))
        cut = slice(i * width, (i + 1) * width)
        picked = picked + dot(mask(own & here), hidden[own_rows, cut]) + dot(mask(other & here), hidden[other_rows, cut])
    active = 0.5 * picked * (1.0 + lax.erf(picked * np.float32(math.sqrt(0.5))))

    for k in range(lane_count):
        cut = slice(k * group, (k + 1) * group)
        payloads[k][:, :width] = active[cut].astype(BF16)
        payloads[k][:, width:] = grad_rows[cut].astype(BF16)
    first = picker(slots, rows, group, cap, 0)
    send_table[...] = dot(first, mask(own)).astype(BF16)
    place_table[...] = dot(first, mask(taken)).astype(BF16)


def merge_kernel(lane_count, cap, *refs):
    got_refs, sent_refs = (refs[0],) + refs[lane_count : 2 * lane_count - 1], refs[:lane_count]
    weight, own, other, grad_rows = refs[2 * lane_count - 1 :]
    group = refs[0].shape[0]
    rows = lane_count * group
    slots = lane_count * cap
    grad_width = grad_rows.shape[1] // (group // cap)
    width = refs[0].shape[1] - grad_width
    got = jnp.concatenate([ref[...] for ref in got_refs], axis=0)
    sent = jnp.concatenate([ref[...] for ref in sent_refs], axis=0)

    def unfold(table, first, step, cols):
        pieces = [dot(picker(slots, rows, group, cap, i), table[:, cols]) for i in range(first, group, step)]
        return jnp.concatenate(pieces, axis=1).astype(BF16)

    merged = slice(0, width)
    picked = jnp.concatenate(
        [unfold(table, first, 2 * cap, merged) for first in (0, cap) for table in (got, sent)], axis=0
    )
    grad_rows[:slots] = unfold(sent, 0, cap, slice(width, width + grad_width))
    grad_rows[slots:] = unfold(got, 0, cap, slice(width, width + grad_width))
    cols = weight.shape[1]
    step = min(512, cols)
    for c in range(0, cols, step):
        total = dot(picked, weight[:, c : c + step])
        own[:, c : c + step] = total[: 2 * slots]
        other[:, c : c + step] = total[2 * slots :].astype(BF16)


def slot_kernel(
    tp_count, own, other, bias, gain, weight, grad_rows, text_sums, text_part, first_part, rows, text_total, *messages
):
    text_total[...] = text_part[...] + first_part[...].astype(F32)
    slots2 = own.shape[0]
    slots = slots2 // 2
    placed = (own[...] + other[...].astype(F32) + bias[...]).astype(BF16)
    rows[...] = placed
    wide = placed.astype(F32)
    squares = jnp.sum(wide * wide, axis=1, keepdims=True)
    scaled = (wide * gain[...]).astype(BF16)
    cols = messages[0].shape[1] - 128
    dots = jnp.zeros_like(squares)
    for k in range(tp_count):
        span = peer_columns("tp", k, cols)
        part = dot(scaled, weight[:, span])
        dots = dots + jnp.sum(part * grad_rows[:, span].astype(F32), axis=1, keepdims=True)
        messages[k][:, :cols] = part[:slots].astype(BF16)
    lane = iota((slots2, 128), 1)
    columns = jnp.where(lane == 0, squares, jnp.where(lane == 1, dots, 0.0))
    padded = round_up(slots2, 128)
    if padded > slots2:
        columns = jnp.concatenate([columns, jnp.zeros((padded - slots2, 128), F32)], axis=0)
    turned = columns.T
    pieces = []
    for i in range(2):
        total = jnp.concatenate([text_sums[i : i + 1], turned[i : i + 1]], axis=1)
        high = total.astype(BF16).astype(F32)
        pieces += [high, total - high]
    line = jnp.concatenate(pieces, axis=1)
    message = jnp.zeros((slots, 128), F32)
    sublane = iota((slots, 128), 0)
    for i in range(line.shape[1] // 128):
        message = jnp.where(sublane == i, line[:, i * 128 : (i + 1) * 128], message)
    for k in range(tp_count):
        messages[k][:, cols:] = message.astype(BF16)


def grad_kernel(grad, grad_rows, weight, gain, text, rows, place_table, out, stream):
    slots = grad_rows.shape[0] // 2
    joined = jnp.concatenate([grad[...], grad_rows[slots:]], axis=0)
    taken = dot_dims(place_table[...], jnp.ones((slots, 128), BF16), 0, 0)[:, 0:1] > 0.0
    step = min(512, weight.shape[0])
    for c in range(0, weight.shape[0], step):
        cut = slice(c, c + step)
        out[:, cut] = gain[:, cut] * dot_dims(joined, weight[cut, :], 1, 1)
        placed = dot_dims(place_table[...], rows[:slots, cut], 0, 0)
        stream[:, cut] = jnp.where(taken, placed, text[:, cut].astype(F32)).astype(BF16)


def final_kernel(tp_count, arrived_count, features, rows, scaled_grad, stream, place_table, send_table, *refs):
    messages, parts = refs[:tp_count], refs[tp_count : tp_count + arrived_count]
    key_value, embed_grad, image_grad, kv_buffer, embed_buffer, image_buffer, sem = refs[tp_count + arrived_count :]
    slots2 = rows.shape[0]
    slots = slots2 // 2
    tokens, cols = kv_buffer.shape
    total = messages[0][...].astype(F32)
    for message in messages[1:]:
        total = total + message[...].astype(F32)
    span = tokens + round_up(slots2, 128)
    line = jnp.concatenate([total[i : i + 1, cols:] for i in range(4 * span // 128)], axis=1)
    squares = line[:, :span] + line[:, span : 2 * span]
    dots = line[:, 2 * span : 3 * span] + line[:, 3 * span :]
    inv = lax.rsqrt(squares / features + EPSILON)
    slope = inv * inv * inv * dots / features
    sublane = iota((128, span), 0)
    turned = jnp.where(sublane == 0, inv, jnp.where(sublane == 1, slope, 0.0)).T
    slot_inv, slot_slope = turned[tokens : tokens + slots2, 0:1], turned[tokens : tokens + slots2, 1:2]
    table = place_table[...].astype(F32)
    taken = jnp.sum(table, axis=0, keepdims=True) > 0.0
    token_inv = jnp.where(taken, jnp.sum(table * slot_inv[:slots], axis=0, keepdims=True), inv[:, :tokens])
    token_slope = jnp.where(taken, jnp.sum(table * slot_slope[:slots], axis=0, keepdims=True), slope[:, :tokens])
    sublane = iota((128, tokens), 0)
    lines = jnp.where(sublane == 0, token_inv, jnp.where(sublane == 1, token_slope, 0.0))
    turned = jnp.where(sublane == 2, taken.astype(F32), lines).T
    inv_col, slope_col, taken_col = turned[:, 0:1], turned[:, 1:2], turned[:, 2:3] > 0.0

    copies = []

    def send(source, target):
        copy = pltpu.make_async_copy(source, target, sem.at[len(copies)])
        copy.start()
        copies.append(copy)

    step = stream.shape[1] // 2
    for c in range(0, stream.shape[1], step):
        cut = slice(c, c + step)
        embed_buffer[:, cut] = (inv_col * scaled_grad[:tokens, cut] - stream[:, cut].astype(F32) * slope_col).astype(BF16)
        send(embed_buffer.at[:, cut], embed_grad.at[:, cut])
        row_grad = slot_inv[slots:] * scaled_grad[tokens:, cut] - rows[slots:, cut].astype(F32) * slot_slope[slots:]
        image_buffer[:, cut] = dot_dims(send_table[...], row_grad.astype(BF16), 0, 0).astype(BF16)
        send(image_buffer.at[:, cut], image_grad.at[:, cut])
    kv_rows = (total[:, :cols] * slot_inv[:slots]).astype(BF16)
    kv_total = parts[0][...]
    for part in parts[1:]:
        kv_total = kv_total + part[...].astype(F32)
    kv_buffer[...] = jnp.where(taken_col, dot_dims(place_table[...], kv_rows, 0, 0), kv_total * inv_col).astype(BF16)
    send(kv_buffer, key_value)
    for copy in copies:
        copy.wait()


def params(mib=16):
    return pltpu.CompilerParams(vmem_limit_bytes=mib * MIB)


def cost_of(flops):
    return pl.CostEstimate(flops=flops, bytes_accessed=1024, transcendentals=0)


COST = cost_of(1024)
MERGE_COST = cost_of(1024)
GRAD_COST = cost_of(1000000000)
TEXT_COST = cost_of(1024)
GATHER_COST = cost_of(4000000000)


def shape(dims, dtype):
    return jax.ShapeDtypeStruct(dims, dtype)


def call(kernel, name, operands, in_specs, outs, out_specs=None, scratch=(), cost=COST):
    return pl.pallas_call(
        kernel,
        out_shape=outs,
        in_specs=in_specs,
        out_specs=out_specs or [VMEM] * len(outs),
        scratch_shapes=scratch,
        compiler_params=params(),
        cost_estimate=cost,
        name=name,
    )(*operands)


def in_hbm(array):
    return pltpu.with_memory_space_constraint(array, pltpu.HBM)


def swap(array, axis, k):
    return lax.ppermute(array, axis, [(i, i ^ k) for i in range(lax.axis_size(axis))])


def on_device(
    merge_hidden, merge_weight, merge_bias, row_dest, image_pos, text_embed, norm_gain, kv_weight, kv_grad
):
    lane_count, tp_count = lax.axis_size("lane"), lax.axis_size("tp")
    tokens, features = text_embed.shape
    kv_cols = kv_weight.shape[1]
    cols = kv_cols // tp_count
    cap = image_pos.shape[3]
    slots = lane_count * cap
    slots2 = 2 * slots
    group = max(16, 2 * cap)
    width = merge_hidden.shape[1] // (group // (2 * cap)) + kv_cols // (group // cap)
    block = row_dest.shape[0]
    gain = norm_gain.reshape(1, features)
    bias = merge_bias.reshape(1, features)
    own_dest = row_dest.reshape(1, block)
    positions = image_pos.reshape(lane_count, cap)

    other_dest = swap(own_dest, "section", 1)
    half = tp_count // 2
    first_part, scaled, text = call(
        lambda *refs: first_text_kernel(half, *refs),
        "first_text_kv",
        [in_hbm(array) for array in (text_embed, gain, kv_weight)],
        [ANY] * 3,
        [shape((tokens, cols), BF16), shape((tokens, features), BF16), pltpu.VMEM(text_embed.shape, BF16)],
        scratch=[
            pltpu.VMEM((1, features), F32),
            pltpu.VMEM((features, cols), BF16),
            pltpu.SemaphoreType.DMA((9,)),
        ],
    )
    first_part, other_dest = lax.optimization_barrier((first_part, other_dest))
    first_arrived = swap(first_part, "tp", half)

    *sent, send_table, place_table = call(
        lambda *refs: gather_kernel(lane_count, group, cap, *refs),
        "gather_rows",
        [other_dest, in_hbm(own_dest), in_hbm(positions), kv_grad, merge_hidden],
        [VMEM, ANY, ANY, VMEM, VMEM],
        [shape((group, width), BF16)] * lane_count
        + [shape((slots, block), BF16), shape((slots, tokens), BF16)],
        scratch=[
            pltpu.VMEM(own_dest.shape, jnp.int32),
            pltpu.VMEM(positions.shape, jnp.int32),
            pltpu.SemaphoreType.DMA((2,)),
        ],
        cost=GATHER_COST,
    )
    send_table, kv_weight, merge_weight = lax.optimization_barrier((send_table, kv_weight, merge_weight))
    got = [swap(sent[k], "lane", k) for k in range(1, lane_count)]

    steps = [k for k in range(1, tp_count) if k != half] + [0]
    *parts, text_own, text_sums = call(
        lambda *refs: text_kernel(half, steps, *refs),
        "text_kv",
        [scaled, kv_weight, kv_grad, text, first_part],
        [VMEM] * 5,
        [shape((tokens, cols), BF16)] * (tp_count - 2) + [shape((tokens, cols), F32), shape((8, tokens), F32)],
        cost=TEXT_COST,
    )
    arrived = [swap(part, "tp", k) for part, k in zip(parts, steps)]

    own, other, grad_rows = call(
        lambda *refs: merge_kernel(lane_count, cap, *refs),
        "merge_rows",
        [*sent, *got, merge_weight],
        [VMEM] * (2 * lane_count),
        [shape((slots2, features), F32), shape((slots2, features), BF16), shape((slots2, kv_cols), BF16)],
        cost=MERGE_COST,
    )
    other = swap(other, "section", 1)

    placed, text_total, *messages = call(
        lambda *refs: slot_kernel(tp_count, *refs),
        "slot_kv",
        [own, other, bias, gain, kv_weight, grad_rows, text_sums, text_own, first_arrived],
        [VMEM] * 9,
        [shape((slots2, features), BF16), shape((tokens, cols), F32)]
        + [shape((slots, cols + 128), BF16)] * tp_count,
    )
    messages = [messages[0]] + [swap(messages[k], "tp", k) for k in range(1, tp_count)]

    scaled_grad, stream = call(
        grad_kernel,
        "normed_grad",
        [kv_grad, grad_rows, kv_weight, gain, text, placed, place_table],
        [VMEM] * 7,
        [shape((tokens + slots, features), F32), shape((tokens, features), BF16)],
        cost=GRAD_COST,
    )

    key_value, embed_grad, image_grad = call(
        lambda *refs: final_kernel(tp_count, tp_count - 1, features * tp_count, *refs),
        "outputs",
        [placed, scaled_grad, stream, place_table, send_table, *messages, text_total, *arrived],
        [VMEM] * (4 + 2 * tp_count),
        [shape((tokens, cols), BF16), shape((tokens, features), BF16), shape((block, features), BF16)],
        out_specs=[ANY] * 3,
        scratch=[
            pltpu.VMEM((tokens, cols), BF16),
            pltpu.VMEM((tokens, features), BF16),
            pltpu.VMEM((block, features), BF16),
            pltpu.SemaphoreType.DMA((5,)),
        ],
    )
    return (key_value, embed_grad, image_grad)


def solution(mesh):
    in_specs = (
        P("lane", "section"),
        P("section", "tp"),
        P("tp"),
        P(("lane", "section")),
        P("lane", "section", None, None),
        P(("lane", "section"), "tp"),
        P("tp"),
        P("tp", None),
        P(("lane", "section"), None),
    )
    out_specs = (
        P(("lane", "section"), "tp"),
        P(("lane", "section"), "tp"),
        P(("lane", "section"), "tp"),
    )
    return jax.shard_map(
        on_device, mesh=mesh, in_specs=in_specs, out_specs=out_specs, check_vma=False
    )
```

```python
import math

import jax
import jax.numpy as jnp
import numpy as np
from jax import lax
from jax.experimental import pallas as pl
from jax.experimental.pallas import tpu as pltpu
from jax.sharding import PartitionSpec as P

EPSILON = 1e-06
F32 = jnp.float32
BF16 = jnp.bfloat16
MIB = 1 << 20
VMEM = pl.BlockSpec(memory_space=pltpu.VMEM)
ANY = pl.BlockSpec(memory_space=pl.ANY)


def round_up(value, step):
    return -(-value // step) * step


def dot(a, b):
    return jnp.dot(a, b, preferred_element_type=F32)


def dot_dims(a, b, dim_a, dim_b):
    return lax.dot_general(a, b, (((dim_a,), (dim_b,)), ((), ())), preferred_element_type=F32)


def iota(shape, dim):
    return lax.broadcasted_iota(jnp.int32, shape, dim)


def one_hot(column, width):
    return (column == iota((column.shape[0], width), 1)).astype(F32).astype(BF16)


def peer_columns(axis, k, cols):
    return pl.ds(pl.multiple_of((lax.axis_index(axis) ^ k) * cols, cols), cols)


def in_middle(dims):
    place = jnp.full(dims, lax.axis_index("tp"), jnp.int32)
    return (place == 1) | (place == 2)


def picker(slots, rows, group, cap, first):
    row = iota((slots, rows), 1)
    place = (row & (group - 1)) - first
    slot = (row >> int(math.log2(group))) * cap + place
    return ((slot == iota((slots, rows), 0)) & (place >= 0) & (place < cap)).astype(F32).astype(BF16)


def mask(match):
    return match.astype(F32).astype(BF16)


def first_text_kernel(step, text_hbm, gain_hbm, weight_hbm, dest_hbm, pos_hbm, part, scaled, text, dest, pos, gain, weight, sem):
    span = peer_columns("tp", step, part.shape[1])
    count = CHUNKS if text.shape[1] % 512 == 0 else 1
    size = text.shape[1] // count
    cuts = [slice(i * size, (i + 1) * size) for i in range(count)]
    copies = []
    for i, cut in enumerate(cuts):
        pair = (
            pltpu.make_async_copy(text_hbm.at[:, cut], text.at[:, cut], sem.at[2 * i + 1]),
            pltpu.make_async_copy(weight_hbm.at[cut, span], weight.at[cut], sem.at[2 * i + 2]),
        )
        for copy in pair:
            copy.start()
        copies.append(pair)
        if i == 0:
            gain_copy = pltpu.make_async_copy(gain_hbm, gain, sem.at[0])
            gain_copy.start()
    small = [pltpu.make_async_copy(*pair, sem.at[2 * count + 1 + i]) for i, pair in enumerate([(dest_hbm, dest), (pos_hbm, pos)])]
    for copy in small:
        copy.start()
    gain_copy.wait()
    total = jnp.zeros(part.shape, F32)
    for cut, pair in zip(cuts, copies):
        pair[0].wait()
        scaled[:, cut] = (text[:, cut].astype(F32) * gain[:, cut]).astype(BF16)
        pair[1].wait()
        total = total + dot(scaled[:, cut], weight[cut])
    part[...] = total.astype(BF16)
    for copy in small:
        copy.wait()


def text_kernel(first_step, steps, scaled, weight, grad, text, first_part, *refs):
    parts, sums = refs[:-1], refs[-1]
    cols = parts[0].shape[1]

    def row_dots(product, span):
        return jnp.sum(product * grad[:, span].astype(F32), axis=1, keepdims=True)

    dots = row_dots(first_part[...].astype(F32), peer_columns("tp", first_step, cols))
    for step, part in zip(steps, parts):
        span = peer_columns("tp", step, cols)
        product = dot(scaled[...], weight[:, span])
        part[...] = product.astype(part.dtype)
        dots = dots + row_dots(product, span)
    wide = text[...].astype(F32)
    squares = jnp.sum(wide * wide, axis=1, keepdims=True)
    lane = iota((text.shape[0], 128), 1)
    sums[...] = jnp.where(lane == 0, squares, jnp.where(lane == 1, dots, 0.0)).T[:8]


def forward_kernel(turned, part, onward):
    added = jnp.where(in_middle(part.shape), turned[...].astype(F32), 0.0)
    onward[...] = (part[...].astype(F32) + added).astype(BF16)


def gather_kernel(lane_count, group, cap, other_ref, own_ref, pos_ref, grad, hidden, *refs):
    payloads, (send_table, place_table) = refs[:lane_count], refs[lane_count:]
    rows = lane_count * group
    slots = lane_count * cap
    block, tokens = own_ref.shape[1], grad.shape[0]
    lane = lax.axis_index("lane")
    row_id = iota((rows, block), 0)
    lane_id = (row_id >> int(math.log2(group))) ^ lane
    place = row_id & (group - 1)
    entry = place & (2 * cap - 1)
    earlier = mask(iota((block, block), 0) < iota((block, block), 1))

    def select(dest, first):
        match = dest == lane_id
        rank = dot(mask(match), earlier)
        return match & (rank == (entry - first).astype(F32))

    own = select(own_ref[...], 0)
    other = select(other_ref[...], cap)
    lane_pick = mask((iota((rows, lane_count), 0) >> int(math.log2(group))) ^ lane == iota((rows, lane_count), 1))
    high, low = pos_ref[...] >> 7, pos_ref[...] & 127
    spread = dot(lane_pick, high.astype(F32).astype(BF16)) * 128.0 + dot(lane_pick, low.astype(F32).astype(BF16))
    chosen = (iota((rows, cap), 0) & (cap - 1)) == iota((rows, cap), 1)
    row_pos = jnp.sum(jnp.where(chosen, spread, 0.0), axis=1, keepdims=True)
    taken = row_pos == iota((rows, tokens), 1).astype(F32)
    taken_place = iota((rows, tokens), 0) & (group - 1)
    grad_folds = group // cap
    grad_width = grad.shape[1] // grad_folds
    grad_rows = jnp.zeros((rows, grad_width), F32)
    for i in range(grad_folds):
        here = (taken_place >= cap * i) & (taken_place < cap * (i + 1))
        grad_rows = grad_rows + dot(mask(taken & here), grad[:, i * grad_width : (i + 1) * grad_width])
    section = lax.axis_index("section")
    own_rows = pl.ds(pl.multiple_of(section * block, block), block)
    other_rows = pl.ds(pl.multiple_of((1 - section) * block, block), block)
    folds = group // (2 * cap)
    width = hidden.shape[1] // folds
    picked = jnp.zeros((rows, width), F32)
    for i in range(folds):
        here = (place >= 2 * cap * i) & (place < 2 * cap * (i + 1))
        cut = slice(i * width, (i + 1) * width)
        picked = picked + dot(mask(own & here), hidden[own_rows, cut]) + dot(mask(other & here), hidden[other_rows, cut])
    active = 0.5 * picked * (1.0 + lax.erf(picked * np.float32(math.sqrt(0.5))))

    for k in range(lane_count):
        cut = slice(k * group, (k + 1) * group)
        payloads[k][:, :width] = active[cut].astype(BF16)
        payloads[k][:, width:] = grad_rows[cut].astype(BF16)
    first = picker(slots, rows, group, cap, 0)
    send_table[...] = dot(first, mask(own)).astype(BF16)
    place_table[...] = dot(first, mask(taken)).astype(BF16)


def merge_kernel(lane_count, cap, *refs):
    got_refs, sent_refs = (refs[0],) + refs[lane_count : 2 * lane_count - 1], refs[:lane_count]
    weight, own, other, grad_rows = refs[2 * lane_count - 1 :]
    group = refs[0].shape[0]
    rows = lane_count * group
    slots = lane_count * cap
    grad_width = grad_rows.shape[1] // (group // cap)
    width = refs[0].shape[1] - grad_width
    got = jnp.concatenate([ref[...] for ref in got_refs], axis=0)
    sent = jnp.concatenate([ref[...] for ref in sent_refs], axis=0)

    def unfold(table, first, step, cols):
        pieces = [dot(picker(slots, rows, group, cap, i), table[:, cols]) for i in range(first, group, step)]
        return jnp.concatenate(pieces, axis=1).astype(BF16)

    merged = slice(0, width)
    picked = jnp.concatenate(
        [unfold(table, first, 2 * cap, merged) for first in (0, cap) for table in (got, sent)], axis=0
    )
    grad_rows[:slots] = unfold(sent, 0, cap, slice(width, width + grad_width))
    grad_rows[slots:] = unfold(got, 0, cap, slice(width, width + grad_width))
    cols = weight.shape[1]
    step = min(512, cols)
    for c in range(0, cols, step):
        total = dot(picked, weight[:, c : c + step])
        own[:, c : c + step] = total[: 2 * slots]
        other[:, c : c + step] = total[2 * slots :].astype(BF16)


def slot_kernel(
    tp_count, own, other, bias, gain, weight, grad_rows, text_sums, text_part, first_arrived, rows, text_total, *messages
):
    arrived = first_arrived[...].astype(F32)
    if tp_count == 4:
        arrived = jnp.where(in_middle(arrived.shape), arrived, 0.0)
    text_total[...] = text_part[...] + arrived
    slots2 = own.shape[0]
    slots = slots2 // 2
    placed = (own[...] + other[...].astype(F32) + bias[...]).astype(BF16)
    rows[...] = placed
    wide = placed.astype(F32)
    squares = jnp.sum(wide * wide, axis=1, keepdims=True)
    scaled = (wide * gain[...]).astype(BF16)
    cols = messages[0].shape[1] - 128
    dots = jnp.zeros_like(squares)
    for k in range(tp_count):
        span = peer_columns("tp", k, cols)
        part = dot(scaled, weight[:, span])
        dots = dots + jnp.sum(part * grad_rows[:, span].astype(F32), axis=1, keepdims=True)
        messages[k][:, :cols] = part[:slots].astype(BF16)
    lane = iota((slots2, 128), 1)
    columns = jnp.where(lane == 0, squares, jnp.where(lane == 1, dots, 0.0))
    padded = round_up(slots2, 128)
    if padded > slots2:
        columns = jnp.concatenate([columns, jnp.zeros((padded - slots2, 128), F32)], axis=0)
    turned = columns.T
    pieces = []
    for i in range(2):
        total = jnp.concatenate([text_sums[i : i + 1], turned[i : i + 1]], axis=1)
        high = total.astype(BF16).astype(F32)
        pieces += [high, total - high]
    line = jnp.concatenate(pieces, axis=1)
    message = jnp.zeros((slots, 128), F32)
    sublane = iota((slots, 128), 0)
    for i in range(line.shape[1] // 128):
        message = jnp.where(sublane == i, line[:, i * 128 : (i + 1) * 128], message)
    for k in range(tp_count):
        messages[k][:, cols:] = message.astype(BF16)


def grad_kernel(grad, grad_rows, weight, gain, text, rows, place_table, out, stream):
    slots = grad_rows.shape[0] // 2
    joined = jnp.concatenate([grad[...], grad_rows[slots:]], axis=0)
    taken = dot_dims(place_table[...], jnp.ones((slots, 128), BF16), 0, 0)[:, 0:1] > 0.0
    step = min(512, weight.shape[0])
    for c in range(0, weight.shape[0], step):
        cut = slice(c, c + step)
        out[:, cut] = gain[:, cut] * dot_dims(joined, weight[cut, :], 1, 1)
        placed = dot_dims(place_table[...], rows[:slots, cut], 0, 0)
        stream[:, cut] = jnp.where(taken, placed, text[:, cut].astype(F32)).astype(BF16)


def final_kernel(tp_count, arrived_count, features, rows, scaled_grad, stream, place_table, send_table, *refs):
    messages, parts = refs[:tp_count], refs[tp_count : tp_count + arrived_count]
    key_value, embed_grad, image_grad, kv_buffer, embed_buffer, image_buffer, sem = refs[tp_count + arrived_count :]
    slots2 = rows.shape[0]
    slots = slots2 // 2
    tokens, cols = kv_buffer.shape
    total = messages[0][...].astype(F32)
    for message in messages[1:]:
        total = total + message[...].astype(F32)
    span = tokens + round_up(slots2, 128)
    line = jnp.concatenate([total[i : i + 1, cols:] for i in range(4 * span // 128)], axis=1)
    squares = line[:, :span] + line[:, span : 2 * span]
    dots = line[:, 2 * span : 3 * span] + line[:, 3 * span :]
    inv = lax.rsqrt(squares / features + EPSILON)
    slope = inv * inv * inv * dots / features
    sublane = iota((128, span), 0)
    turned = jnp.where(sublane == 0, inv, jnp.where(sublane == 1, slope, 0.0)).T
    slot_inv, slot_slope = turned[tokens : tokens + slots2, 0:1], turned[tokens : tokens + slots2, 1:2]
    table = place_table[...].astype(F32)
    taken = jnp.sum(table, axis=0, keepdims=True) > 0.0
    token_inv = jnp.where(taken, jnp.sum(table * slot_inv[:slots], axis=0, keepdims=True), inv[:, :tokens])
    token_slope = jnp.where(taken, jnp.sum(table * slot_slope[:slots], axis=0, keepdims=True), slope[:, :tokens])
    sublane = iota((128, tokens), 0)
    lines = jnp.where(sublane == 0, token_inv, jnp.where(sublane == 1, token_slope, 0.0))
    turned = jnp.where(sublane == 2, taken.astype(F32), lines).T
    inv_col, slope_col, taken_col = turned[:, 0:1], turned[:, 1:2], turned[:, 2:3] > 0.0

    copies = []

    def send(source, target):
        copy = pltpu.make_async_copy(source, target, sem.at[len(copies)])
        copy.start()
        copies.append(copy)

    step = max(128, stream.shape[1] // PIECES)
    for c in range(0, stream.shape[1], step):
        cut = slice(c, c + step)
        embed_buffer[:, cut] = (inv_col * scaled_grad[:tokens, cut] - stream[:, cut].astype(F32) * slope_col).astype(BF16)
        send(embed_buffer.at[:, cut], embed_grad.at[:, cut])
        row_grad = slot_inv[slots:] * scaled_grad[tokens:, cut] - rows[slots:, cut].astype(F32) * slot_slope[slots:]
        image_buffer[:, cut] = dot_dims(send_table[...], row_grad.astype(BF16), 0, 0).astype(BF16)
        send(image_buffer.at[:, cut], image_grad.at[:, cut])
    kv_rows = (total[:, :cols] * slot_inv[:slots]).astype(BF16)
    kv_total = parts[0][...]
    for part in parts[1:]:
        kv_total = kv_total + part[...].astype(F32)
    kv_buffer[...] = jnp.where(taken_col, dot_dims(place_table[...], kv_rows, 0, 0), kv_total * inv_col).astype(BF16)
    send(kv_buffer, key_value)
    for copy in copies:
        copy.wait()


def params(mib=16):
    return pltpu.CompilerParams(vmem_limit_bytes=mib * MIB)


def cost_of(flops):
    return pl.CostEstimate(flops=flops, bytes_accessed=1024, transcendentals=0)


COST = cost_of(1024)
CHUNKS = 4
PIECES = 2
MERGE_COST = cost_of(1024)
GRAD_COST = cost_of(1000000000)
TEXT_COST = cost_of(1024)
SLOT_COST = cost_of(1024)
GATHER_COST = cost_of(4000000000)


def shape(dims, dtype):
    return jax.ShapeDtypeStruct(dims, dtype)


def call(kernel, name, operands, in_specs, outs, out_specs=None, scratch=(), cost=COST):
    return pl.pallas_call(
        kernel,
        out_shape=outs,
        in_specs=in_specs,
        out_specs=out_specs or [VMEM] * len(outs),
        scratch_shapes=scratch,
        compiler_params=params(),
        cost_estimate=cost,
        name=name,
    )(*operands)


def in_hbm(array):
    return pltpu.with_memory_space_constraint(array, pltpu.HBM)


def swap(array, axis, k):
    return lax.ppermute(array, axis, [(i, i ^ k) for i in range(lax.axis_size(axis))])


def on_device(
    merge_hidden, merge_weight, merge_bias, row_dest, image_pos, text_embed, norm_gain, kv_weight, kv_grad
):
    lane_count, tp_count = lax.axis_size("lane"), lax.axis_size("tp")
    tokens, features = text_embed.shape
    kv_cols = kv_weight.shape[1]
    cols = kv_cols // tp_count
    cap = image_pos.shape[3]
    slots = lane_count * cap
    slots2 = 2 * slots
    group = max(16, 2 * cap)
    width = merge_hidden.shape[1] // (group // (2 * cap)) + kv_cols // (group // cap)
    block = row_dest.shape[0]
    gain = norm_gain.reshape(1, features)
    bias = merge_bias.reshape(1, features)
    own_dest = row_dest.reshape(1, block)
    positions = image_pos.reshape(lane_count, cap)

    first = 3 if tp_count == 4 else tp_count // 2
    first_part, scaled, text, own_dest, positions = call(
        lambda *refs: first_text_kernel(first, *refs),
        "first_text_kv",
        [in_hbm(array) for array in (text_embed, gain, kv_weight, own_dest, positions)],
        [ANY] * 5,
        [shape((tokens, cols), BF16), shape((tokens, features), BF16)]
        + [pltpu.VMEM(array.shape, array.dtype) for array in (text_embed, own_dest, positions)],
        scratch=[
            pltpu.VMEM((1, features), F32),
            pltpu.VMEM((features, cols), BF16),
            pltpu.SemaphoreType.DMA((2 * CHUNKS + 3,)),
        ],
    )
    if tp_count == 4:
        turned = swap(first_part, "tp", 1)
        sections = lax.axis_size("section")
        pairs = [
            (section * 4 + z, section * 4 + 3 - z if z in (1, 2) else (section + 1) % sections * 4 + z)
            for section in range(sections)
            for z in range(4)
        ]
        first_arrived = lax.ppermute(first_part, ("section", "tp"), pairs)
    else:
        first_arrived = swap(first_part, "tp", first)

    other_dest = swap(own_dest, "section", 1)
    *sent, send_table, place_table = call(
        lambda *refs: gather_kernel(lane_count, group, cap, *refs),
        "gather_rows",
        [other_dest, own_dest, positions, kv_grad, merge_hidden],
        [VMEM] * 5,
        [shape((group, width), BF16)] * lane_count
        + [shape((slots, block), BF16), shape((slots, tokens), BF16)],
        cost=GATHER_COST,
    )
    send_table, kv_weight, merge_weight = lax.optimization_barrier((send_table, kv_weight, merge_weight))
    got = [swap(sent[k], "lane", k) for k in range(1, lane_count)]

    steps = [k for k in range(tp_count - 1, 0, -1) if k != first] + [0]
    *parts, text_own, text_sums = call(
        lambda *refs: text_kernel(first, steps, *refs),
        "text_kv",
        [scaled, kv_weight, kv_grad, text, first_part],
        [VMEM] * 5,
        [shape((tokens, cols), BF16)] * (tp_count - 2) + [shape((tokens, cols), F32), shape((8, tokens), F32)],
        cost=TEXT_COST,
    )
    if tp_count == 4:
        (parts[0],) = call(forward_kernel, "forward", [turned, parts[0]], [VMEM] * 2, [shape((tokens, cols), BF16)])
        parts = list(lax.optimization_barrier(tuple(parts)))
    arrived = [swap(part, "tp", k) for part, k in zip(parts, steps)]

    own, other, grad_rows = call(
        lambda *refs: merge_kernel(lane_count, cap, *refs),
        "merge_rows",
        [*sent, *got, merge_weight],
        [VMEM] * (2 * lane_count),
        [shape((slots2, features), F32), shape((slots2, features), BF16), shape((slots2, kv_cols), BF16)],
        cost=MERGE_COST,
    )
    other = swap(other, "section", 1)

    placed, text_total, *messages = call(
        lambda *refs: slot_kernel(tp_count, *refs),
        "slot_kv",
        [own, other, bias, gain, kv_weight, grad_rows, text_sums, text_own, first_arrived],
        [VMEM] * 9,
        [shape((slots2, features), BF16), shape((tokens, cols), F32)]
        + [shape((slots, cols + 128), BF16)] * tp_count,
        cost=SLOT_COST,
    )
    messages = [messages[0]] + [swap(messages[k], "tp", k) for k in range(1, tp_count)]

    scaled_grad, stream = call(
        grad_kernel,
        "normed_grad",
        [kv_grad, grad_rows, kv_weight, gain, text, placed, place_table],
        [VMEM] * 7,
        [shape((tokens + slots, features), F32), shape((tokens, features), BF16)],
        cost=GRAD_COST,
    )

    key_value, embed_grad, image_grad = call(
        lambda *refs: final_kernel(tp_count, tp_count - 1, features * tp_count, *refs),
        "outputs",
        [placed, scaled_grad, stream, place_table, send_table, *messages, text_total, *arrived],
        [VMEM] * (4 + 2 * tp_count),
        [shape((tokens, cols), BF16), shape((tokens, features), BF16), shape((block, features), BF16)],
        out_specs=[ANY] * 3,
        scratch=[
            pltpu.VMEM((tokens, cols), BF16),
            pltpu.VMEM((tokens, features), BF16),
            pltpu.VMEM((block, features), BF16),
            pltpu.SemaphoreType.DMA((2 * PIECES + 1,)),
        ],
    )
    return (key_value, embed_grad, image_grad)


def solution(mesh):
    in_specs = (
        P("lane", "section"),
        P("section", "tp"),
        P("tp"),
        P(("lane", "section")),
        P("lane", "section", None, None),
        P(("lane", "section"), "tp"),
        P("tp"),
        P("tp", None),
        P(("lane", "section"), None),
    )
    out_specs = (
        P(("lane", "section"), "tp"),
        P(("lane", "section"), "tp"),
        P(("lane", "section"), "tp"),
    )
    return jax.shard_map(
        on_device, mesh=mesh, in_specs=in_specs, out_specs=out_specs, check_vma=False
    )
```

```python
import math

import jax
import jax.numpy as jnp
import numpy as np
from jax import lax
from jax.experimental import pallas as pl
from jax.experimental.pallas import tpu as pltpu
from jax.sharding import PartitionSpec as P

EPSILON = 1e-06
F32 = jnp.float32
BF16 = jnp.bfloat16
MIB = 1 << 20
VMEM = pl.BlockSpec(memory_space=pltpu.VMEM)
ANY = pl.BlockSpec(memory_space=pl.ANY)


def round_up(value, step):
    return -(-value // step) * step


def dot(a, b):
    return jnp.dot(a, b, preferred_element_type=F32)


def dot_dims(a, b, dim_a, dim_b):
    return lax.dot_general(a, b, (((dim_a,), (dim_b,)), ((), ())), preferred_element_type=F32)


def iota(shape, dim):
    return lax.broadcasted_iota(jnp.int32, shape, dim)


def one_hot(column, width):
    return (column == iota((column.shape[0], width), 1)).astype(F32).astype(BF16)


def peer_columns(axis, k, cols):
    return pl.ds(pl.multiple_of((lax.axis_index(axis) ^ k) * cols, cols), cols)


def in_middle(dims):
    place = jnp.full(dims, lax.axis_index("tp"), jnp.int32)
    return (place == 1) | (place == 2)


def picker(slots, rows, group, cap, first):
    row = iota((slots, rows), 1)
    place = (row & (group - 1)) - first
    slot = (row >> int(math.log2(group))) * cap + place
    return ((slot == iota((slots, rows), 0)) & (place >= 0) & (place < cap)).astype(F32).astype(BF16)


def mask(match):
    return match.astype(F32).astype(BF16)


def first_text_kernel(step, text_hbm, gain_hbm, weight_hbm, dest_hbm, pos_hbm, part, scaled, text, dest, pos, gain, weight, sem):
    span = peer_columns("tp", step, part.shape[1])
    count = CHUNKS if text.shape[1] % 512 == 0 else 1
    size = text.shape[1] // count
    cuts = [slice(i * size, (i + 1) * size) for i in range(count)]
    copies = []
    for i, cut in enumerate(cuts):
        pair = (
            pltpu.make_async_copy(text_hbm.at[:, cut], text.at[:, cut], sem.at[2 * i + 1]),
            pltpu.make_async_copy(weight_hbm.at[cut, span], weight.at[cut], sem.at[2 * i + 2]),
        )
        for copy in pair:
            copy.start()
        copies.append(pair)
        if i == 0:
            gain_copy = pltpu.make_async_copy(gain_hbm, gain, sem.at[0])
            gain_copy.start()
    small = [pltpu.make_async_copy(*pair, sem.at[2 * count + 1 + i]) for i, pair in enumerate([(dest_hbm, dest), (pos_hbm, pos)])]
    for copy in small:
        copy.start()
    gain_copy.wait()
    total = jnp.zeros(part.shape, F32)
    for cut, pair in zip(cuts, copies):
        pair[0].wait()
        scaled[:, cut] = (text[:, cut].astype(F32) * gain[:, cut]).astype(BF16)
        pair[1].wait()
        total = total + dot(scaled[:, cut], weight[cut])
    part[...] = total.astype(BF16)
    for copy in small:
        copy.wait()


def text_kernel(first_step, steps, scaled, weight, grad, text, first_part, *refs):
    parts, sums = refs[:-1], refs[-1]
    cols = parts[0].shape[1]

    def row_dots(product, span):
        return jnp.sum(product * grad[:, span].astype(F32), axis=1, keepdims=True)

    dots = row_dots(first_part[...].astype(F32), peer_columns("tp", first_step, cols))
    for step, part in zip(steps, parts):
        span = peer_columns("tp", step, cols)
        product = dot(scaled[...], weight[:, span])
        part[...] = product.astype(part.dtype)
        dots = dots + row_dots(product, span)
    wide = text[...].astype(F32)
    squares = jnp.sum(wide * wide, axis=1, keepdims=True)
    lane = iota((text.shape[0], 128), 1)
    sums[...] = jnp.where(lane == 0, squares, jnp.where(lane == 1, dots, 0.0)).T[:8]


def forward_kernel(turned, part, onward):
    added = jnp.where(in_middle(part.shape), turned[...].astype(F32), 0.0)
    onward[...] = (part[...].astype(F32) + added).astype(BF16)


def gather_kernel(lane_count, group, cap, other_ref, own_ref, pos_ref, grad, hidden, *refs):
    payloads, (send_table, place_table) = refs[:lane_count], refs[lane_count:]
    rows = lane_count * group
    slots = lane_count * cap
    block, tokens = own_ref.shape[1], grad.shape[0]
    lane = lax.axis_index("lane")
    row_id = iota((rows, block), 0)
    lane_id = (row_id >> int(math.log2(group))) ^ lane
    place = row_id & (group - 1)
    entry = place & (2 * cap - 1)
    earlier = mask(iota((block, block), 0) < iota((block, block), 1))

    def select(dest, first):
        match = dest == lane_id
        rank = dot(mask(match), earlier)
        return match & (rank == (entry - first).astype(F32))

    own = select(own_ref[...], 0)
    other = select(other_ref[...], cap)
    lane_pick = mask((iota((rows, lane_count), 0) >> int(math.log2(group))) ^ lane == iota((rows, lane_count), 1))
    high, low = pos_ref[...] >> 7, pos_ref[...] & 127
    spread = dot(lane_pick, high.astype(F32).astype(BF16)) * 128.0 + dot(lane_pick, low.astype(F32).astype(BF16))
    chosen = (iota((rows, cap), 0) & (cap - 1)) == iota((rows, cap), 1)
    row_pos = jnp.sum(jnp.where(chosen, spread, 0.0), axis=1, keepdims=True)
    taken = row_pos == iota((rows, tokens), 1).astype(F32)
    taken_place = iota((rows, tokens), 0) & (group - 1)
    grad_folds = group // cap
    grad_width = grad.shape[1] // grad_folds
    grad_rows = jnp.zeros((rows, grad_width), F32)
    for i in range(grad_folds):
        here = (taken_place >= cap * i) & (taken_place < cap * (i + 1))
        grad_rows = grad_rows + dot(mask(taken & here), grad[:, i * grad_width : (i + 1) * grad_width])
    section = lax.axis_index("section")
    own_rows = pl.ds(pl.multiple_of(section * block, block), block)
    other_rows = pl.ds(pl.multiple_of((1 - section) * block, block), block)
    folds = group // (2 * cap)
    width = hidden.shape[1] // folds
    picked = jnp.zeros((rows, width), F32)
    for i in range(folds):
        here = (place >= 2 * cap * i) & (place < 2 * cap * (i + 1))
        cut = slice(i * width, (i + 1) * width)
        picked = picked + dot(mask(own & here), hidden[own_rows, cut]) + dot(mask(other & here), hidden[other_rows, cut])
    active = 0.5 * picked * (1.0 + lax.erf(picked * np.float32(math.sqrt(0.5))))

    for k in range(lane_count):
        cut = slice(k * group, (k + 1) * group)
        payloads[k][:, :width] = active[cut].astype(BF16)
        payloads[k][:, width:] = grad_rows[cut].astype(BF16)
    first = picker(slots, rows, group, cap, 0)
    send_table[...] = dot(first, mask(own)).astype(BF16)
    place_table[...] = dot(first, mask(taken)).astype(BF16)


def merge_kernel(lane_count, cap, *refs):
    got_refs, sent_refs = (refs[0],) + refs[lane_count : 2 * lane_count - 1], refs[:lane_count]
    weight, own, other, grad_rows = refs[2 * lane_count - 1 :]
    group = refs[0].shape[0]
    rows = lane_count * group
    slots = lane_count * cap
    grad_width = grad_rows.shape[1] // (group // cap)
    width = refs[0].shape[1] - grad_width
    got = jnp.concatenate([ref[...] for ref in got_refs], axis=0)
    sent = jnp.concatenate([ref[...] for ref in sent_refs], axis=0)

    def unfold(table, first, step, cols):
        pieces = [dot(picker(slots, rows, group, cap, i), table[:, cols]) for i in range(first, group, step)]
        return jnp.concatenate(pieces, axis=1).astype(BF16)

    merged = slice(0, width)
    picked = jnp.concatenate(
        [unfold(table, first, 2 * cap, merged) for first in (0, cap) for table in (got, sent)], axis=0
    )
    grad_rows[:slots] = unfold(sent, 0, cap, slice(width, width + grad_width))
    grad_rows[slots:] = unfold(got, 0, cap, slice(width, width + grad_width))
    cols = weight.shape[1]
    step = min(512, cols)
    for c in range(0, cols, step):
        total = dot(picked, weight[:, c : c + step])
        own[:, c : c + step] = total[: 2 * slots]
        other[:, c : c + step] = total[2 * slots :].astype(BF16)


def slot_kernel(
    tp_count, own, other, bias, gain, weight, grad_rows, text_sums, text_part, first_arrived, rows, text_total, *messages
):
    arrived = first_arrived[...].astype(F32)
    if tp_count == 4:
        arrived = jnp.where(in_middle(arrived.shape), arrived, 0.0)
    text_total[...] = text_part[...] + arrived
    slots2 = own.shape[0]
    slots = slots2 // 2
    placed = (own[...] + other[...].astype(F32) + bias[...]).astype(BF16)
    rows[...] = placed
    wide = placed.astype(F32)
    squares = jnp.sum(wide * wide, axis=1, keepdims=True)
    scaled = (wide * gain[...]).astype(BF16)
    cols = messages[0].shape[1] - 128
    dots = jnp.zeros_like(squares)
    for k in range(tp_count):
        span = peer_columns("tp", k, cols)
        part = dot(scaled, weight[:, span])
        dots = dots + jnp.sum(part * grad_rows[:, span].astype(F32), axis=1, keepdims=True)
        messages[k][:, :cols] = part[:slots].astype(BF16)
    lane = iota((slots2, 128), 1)
    columns = jnp.where(lane == 0, squares, jnp.where(lane == 1, dots, 0.0))
    padded = round_up(slots2, 128)
    if padded > slots2:
        columns = jnp.concatenate([columns, jnp.zeros((padded - slots2, 128), F32)], axis=0)
    turned = columns.T
    pieces = []
    for i in range(2):
        total = jnp.concatenate([text_sums[i : i + 1], turned[i : i + 1]], axis=1)
        high = total.astype(BF16).astype(F32)
        pieces += [high, total - high]
    line = jnp.concatenate(pieces, axis=1)
    message = jnp.zeros((slots, 128), F32)
    sublane = iota((slots, 128), 0)
    for i in range(line.shape[1] // 128):
        message = jnp.where(sublane == i, line[:, i * 128 : (i + 1) * 128], message)
    for k in range(tp_count):
        messages[k][:, cols:] = message.astype(BF16)


def grad_kernel(grad, grad_rows, weight, gain, text, rows, place_table, out, stream):
    slots = grad_rows.shape[0] // 2
    joined = jnp.concatenate([grad[...], grad_rows[slots:]], axis=0)
    taken = dot_dims(place_table[...], jnp.ones((slots, 128), BF16), 0, 0)[:, 0:1] > 0.0
    step = min(512, weight.shape[0])
    for c in range(0, weight.shape[0], step):
        cut = slice(c, c + step)
        out[:, cut] = gain[:, cut] * dot_dims(joined, weight[cut, :], 1, 1)
        placed = dot_dims(place_table[...], rows[:slots, cut], 0, 0)
        stream[:, cut] = jnp.where(taken, placed, text[:, cut].astype(F32)).astype(BF16)


def final_kernel(tp_count, arrived_count, features, rows, scaled_grad, stream, place_table, send_table, *refs):
    messages, parts = refs[:tp_count], refs[tp_count : tp_count + arrived_count]
    key_value, embed_grad, image_grad, kv_buffer, embed_buffer, image_buffer, sem = refs[tp_count + arrived_count :]
    slots2 = rows.shape[0]
    slots = slots2 // 2
    tokens, cols = kv_buffer.shape
    total = messages[0][...].astype(F32)
    for message in messages[1:]:
        total = total + message[...].astype(F32)
    span = tokens + round_up(slots2, 128)
    line = jnp.concatenate([total[i : i + 1, cols:] for i in range(4 * span // 128)], axis=1)
    squares = line[:, :span] + line[:, span : 2 * span]
    dots = line[:, 2 * span : 3 * span] + line[:, 3 * span :]
    inv = lax.rsqrt(squares / features + EPSILON)
    slope = inv * inv * inv * dots / features
    sublane = iota((128, span), 0)
    turned = jnp.where(sublane == 0, inv, jnp.where(sublane == 1, slope, 0.0)).T
    slot_inv, slot_slope = turned[tokens : tokens + slots2, 0:1], turned[tokens : tokens + slots2, 1:2]
    table = place_table[...].astype(F32)
    taken = jnp.sum(table, axis=0, keepdims=True) > 0.0
    token_inv = jnp.where(taken, jnp.sum(table * slot_inv[:slots], axis=0, keepdims=True), inv[:, :tokens])
    token_slope = jnp.where(taken, jnp.sum(table * slot_slope[:slots], axis=0, keepdims=True), slope[:, :tokens])
    sublane = iota((128, tokens), 0)
    lines = jnp.where(sublane == 0, token_inv, jnp.where(sublane == 1, token_slope, 0.0))
    turned = jnp.where(sublane == 2, taken.astype(F32), lines).T
    inv_col, slope_col, taken_col = turned[:, 0:1], turned[:, 1:2], turned[:, 2:3] > 0.0

    copies = []

    def send(source, target):
        copy = pltpu.make_async_copy(source, target, sem.at[len(copies)])
        copy.start()
        copies.append(copy)

    step = max(128, stream.shape[1] // PIECES)
    for c in range(0, stream.shape[1], step):
        cut = slice(c, c + step)
        embed_buffer[:, cut] = (inv_col * scaled_grad[:tokens, cut] - stream[:, cut].astype(F32) * slope_col).astype(BF16)
        send(embed_buffer.at[:, cut], embed_grad.at[:, cut])
        row_grad = slot_inv[slots:] * scaled_grad[tokens:, cut] - rows[slots:, cut].astype(F32) * slot_slope[slots:]
        image_buffer[:, cut] = dot_dims(send_table[...], row_grad.astype(BF16), 0, 0).astype(BF16)
        send(image_buffer.at[:, cut], image_grad.at[:, cut])
    kv_rows = (total[:, :cols] * slot_inv[:slots]).astype(BF16)
    kv_total = parts[0][...]
    for part in parts[1:]:
        kv_total = kv_total + part[...].astype(F32)
    kv_buffer[...] = jnp.where(taken_col, dot_dims(place_table[...], kv_rows, 0, 0), kv_total * inv_col).astype(BF16)
    send(kv_buffer, key_value)
    for copy in copies:
        copy.wait()


def params(mib=16):
    return pltpu.CompilerParams(vmem_limit_bytes=mib * MIB)


def cost_of(flops):
    return pl.CostEstimate(flops=flops, bytes_accessed=1024, transcendentals=0)


COST = cost_of(1024)
CHUNKS = 4
PIECES = 2
MERGE_COST = cost_of(1024)
GRAD_COST = cost_of(1000000000)
TEXT_COST = cost_of(1024)
SLOT_COST = cost_of(1024)
GATHER_COST = cost_of(4000000000)


def shape(dims, dtype):
    return jax.ShapeDtypeStruct(dims, dtype)


def call(kernel, name, operands, in_specs, outs, out_specs=None, scratch=(), cost=COST):
    return pl.pallas_call(
        kernel,
        out_shape=outs,
        in_specs=in_specs,
        out_specs=out_specs or [VMEM] * len(outs),
        scratch_shapes=scratch,
        compiler_params=params(),
        cost_estimate=cost,
        name=name,
    )(*operands)


def in_hbm(array):
    return pltpu.with_memory_space_constraint(array, pltpu.HBM)


def swap(array, axis, k):
    return lax.ppermute(array, axis, [(i, i ^ k) for i in range(lax.axis_size(axis))])


def on_device(
    merge_hidden, merge_weight, merge_bias, row_dest, image_pos, text_embed, norm_gain, kv_weight, kv_grad
):
    lane_count, tp_count = lax.axis_size("lane"), lax.axis_size("tp")
    tokens, features = text_embed.shape
    kv_cols = kv_weight.shape[1]
    cols = kv_cols // tp_count
    cap = image_pos.shape[3]
    slots = lane_count * cap
    slots2 = 2 * slots
    group = max(16, 2 * cap)
    width = merge_hidden.shape[1] // (group // (2 * cap)) + kv_cols // (group // cap)
    block = row_dest.shape[0]
    gain = norm_gain.reshape(1, features)
    bias = merge_bias.reshape(1, features)
    own_dest = row_dest.reshape(1, block)
    positions = image_pos.reshape(lane_count, cap)

    first = 3 if tp_count == 4 else tp_count // 2
    first_part, scaled, text, own_dest, positions = call(
        lambda *refs: first_text_kernel(first, *refs),
        "first_text_kv",
        [in_hbm(array) for array in (text_embed, gain, kv_weight, own_dest, positions)],
        [ANY] * 5,
        [shape((tokens, cols), BF16), shape((tokens, features), BF16)]
        + [pltpu.VMEM(array.shape, array.dtype) for array in (text_embed, own_dest, positions)],
        scratch=[
            pltpu.VMEM((1, features), F32),
            pltpu.VMEM((features, cols), BF16),
            pltpu.SemaphoreType.DMA((2 * CHUNKS + 3,)),
        ],
    )
    if tp_count == 4:
        turned = swap(first_part, "tp", 1)
        sections = lax.axis_size("section")
        pairs = [
            (section * 4 + z, section * 4 + 3 - z if z in (1, 2) else (section + 1) % sections * 4 + z)
            for section in range(sections)
            for z in range(4)
        ]
        first_arrived = lax.ppermute(first_part, ("section", "tp"), pairs)
    else:
        first_arrived = swap(first_part, "tp", first)

    other_dest = swap(own_dest, "section", 1)
    *sent, send_table, place_table = call(
        lambda *refs: gather_kernel(lane_count, group, cap, *refs),
        "gather_rows",
        [other_dest, own_dest, positions, kv_grad, merge_hidden],
        [VMEM] * 5,
        [shape((group, width), BF16)] * lane_count
        + [shape((slots, block), BF16), shape((slots, tokens), BF16)],
        cost=GATHER_COST,
    )
    send_table, kv_weight, merge_weight = lax.optimization_barrier((send_table, kv_weight, merge_weight))
    got = [swap(sent[k], "lane", k) for k in range(1, lane_count)]

    steps = [k for k in range(tp_count - 1, 0, -1) if k != first] + [0]
    *parts, text_own, text_sums = call(
        lambda *refs: text_kernel(first, steps, *refs),
        "text_kv",
        [scaled, kv_weight, kv_grad, text, first_part],
        [VMEM] * 5,
        [shape((tokens, cols), BF16)] * (tp_count - 2) + [shape((tokens, cols), F32), shape((8, tokens), F32)],
        cost=TEXT_COST,
    )
    if tp_count == 4:
        (parts[0],) = call(forward_kernel, "forward", [turned, parts[0]], [VMEM] * 2, [shape((tokens, cols), BF16)])
        parts = list(lax.optimization_barrier(tuple(parts)))
    arrived = [swap(part, "tp", k) for part, k in zip(parts, steps)]

    own, other, grad_rows = call(
        lambda *refs: merge_kernel(lane_count, cap, *refs),
        "merge_rows",
        [*sent, *got, merge_weight],
        [VMEM] * (2 * lane_count),
        [shape((slots2, features), F32), shape((slots2, features), BF16), shape((slots2, kv_cols), BF16)],
        cost=MERGE_COST,
    )
    other = swap(other, "section", 1)

    placed, text_total, *messages = call(
        lambda *refs: slot_kernel(tp_count, *refs),
        "slot_kv",
        [own, other, bias, gain, kv_weight, grad_rows, text_sums, text_own, first_arrived],
        [VMEM] * 9,
        [shape((slots2, features), BF16), shape((tokens, cols), F32)]
        + [shape((slots, cols + 128), BF16)] * tp_count,
        cost=SLOT_COST,
    )
    messages = [swap(messages[k], "tp", k) for k in range(tp_count - 1, 0, -1)] + [messages[0]]

    scaled_grad, stream = call(
        grad_kernel,
        "normed_grad",
        [kv_grad, grad_rows, kv_weight, gain, text, placed, place_table],
        [VMEM] * 7,
        [shape((tokens + slots, features), F32), shape((tokens, features), BF16)],
        cost=GRAD_COST,
    )

    key_value, embed_grad, image_grad = call(
        lambda *refs: final_kernel(tp_count, tp_count - 1, features * tp_count, *refs),
        "outputs",
        [placed, scaled_grad, stream, place_table, send_table, *messages, text_total, *arrived],
        [VMEM] * (4 + 2 * tp_count),
        [shape((tokens, cols), BF16), shape((tokens, features), BF16), shape((block, features), BF16)],
        out_specs=[ANY] * 3,
        scratch=[
            pltpu.VMEM((tokens, cols), BF16),
            pltpu.VMEM((tokens, features), BF16),
            pltpu.VMEM((block, features), BF16),
            pltpu.SemaphoreType.DMA((2 * PIECES + 1,)),
        ],
    )
    return (key_value, embed_grad, image_grad)


def solution(mesh):
    in_specs = (
        P("lane", "section"),
        P("section", "tp"),
        P("tp"),
        P(("lane", "section")),
        P("lane", "section", None, None),
        P(("lane", "section"), "tp"),
        P("tp"),
        P("tp", None),
        P(("lane", "section"), None),
    )
    out_specs = (
        P(("lane", "section"), "tp"),
        P(("lane", "section"), "tp"),
        P(("lane", "section"), "tp"),
    )
    return jax.shard_map(
        on_device, mesh=mesh, in_specs=in_specs, out_specs=out_specs, check_vma=False
    )
```

```python
import math

import jax
import jax.numpy as jnp
import numpy as np
from jax import lax
from jax.experimental import pallas as pl
from jax.experimental.pallas import tpu as pltpu
from jax.sharding import PartitionSpec as P

EPSILON = 1e-06
F32 = jnp.float32
BF16 = jnp.bfloat16
MIB = 1 << 20
VMEM = pl.BlockSpec(memory_space=pltpu.VMEM)
ANY = pl.BlockSpec(memory_space=pl.ANY)


def round_up(value, step):
    return -(-value // step) * step


def dot(a, b):
    return jnp.dot(a, b, preferred_element_type=F32)


def dot_dims(a, b, dim_a, dim_b):
    return lax.dot_general(a, b, (((dim_a,), (dim_b,)), ((), ())), preferred_element_type=F32)


def iota(shape, dim):
    return lax.broadcasted_iota(jnp.int32, shape, dim)


def one_hot(column, width):
    return (column == iota((column.shape[0], width), 1)).astype(F32).astype(BF16)


def peer_columns(axis, k, cols):
    return pl.ds(pl.multiple_of((lax.axis_index(axis) ^ k) * cols, cols), cols)


def in_middle(dims):
    place = jnp.full(dims, lax.axis_index("tp"), jnp.int32)
    return (place == 1) | (place == 2)


def picker(slots, rows, group, cap, first):
    row = iota((slots, rows), 1)
    place = (row & (group - 1)) - first
    slot = (row >> int(math.log2(group))) * cap + place
    return ((slot == iota((slots, rows), 0)) & (place >= 0) & (place < cap)).astype(F32).astype(BF16)


def mask(match):
    return match.astype(F32).astype(BF16)


def first_text_kernel(step, text_hbm, gain_hbm, weight_hbm, dest_hbm, pos_hbm, part, scaled, text, dest, pos, gain, weight, sem):
    span = peer_columns("tp", step, part.shape[1])
    count = CHUNKS if text.shape[1] % 512 == 0 else 1
    size = text.shape[1] // count
    cuts = [slice(i * size, (i + 1) * size) for i in range(count)]
    copies = []
    for i, cut in enumerate(cuts):
        pair = (
            pltpu.make_async_copy(text_hbm.at[:, cut], text.at[:, cut], sem.at[2 * i + 1]),
            pltpu.make_async_copy(weight_hbm.at[cut, span], weight.at[cut], sem.at[2 * i + 2]),
        )
        for copy in pair:
            copy.start()
        copies.append(pair)
        if i == 0:
            gain_copy = pltpu.make_async_copy(gain_hbm, gain, sem.at[0])
            gain_copy.start()
    small = [pltpu.make_async_copy(*pair, sem.at[2 * count + 1 + i]) for i, pair in enumerate([(dest_hbm, dest), (pos_hbm, pos)])]
    for copy in small:
        copy.start()
    gain_copy.wait()
    total = jnp.zeros(part.shape, F32)
    for cut, pair in zip(cuts, copies):
        pair[0].wait()
        scaled[:, cut] = (text[:, cut].astype(F32) * gain[:, cut]).astype(BF16)
        pair[1].wait()
        total = total + dot(scaled[:, cut], weight[cut])
    part[...] = total.astype(BF16)
    for copy in small:
        copy.wait()


def text_kernel(first_step, steps, scaled, weight, grad, text, first_part, *refs):
    parts, sums = refs[:-1], refs[-1]
    cols = parts[0].shape[1]

    def row_dots(product, span):
        return jnp.sum(product * grad[:, span].astype(F32), axis=1, keepdims=True)

    dots = row_dots(first_part[...].astype(F32), peer_columns("tp", first_step, cols))
    for step, part in zip(steps, parts):
        span = peer_columns("tp", step, cols)
        product = dot(scaled[...], weight[:, span])
        part[...] = product.astype(part.dtype)
        dots = dots + row_dots(product, span)
    wide = text[...].astype(F32)
    squares = jnp.sum(wide * wide, axis=1, keepdims=True)
    lane = iota((text.shape[0], 128), 1)
    sums[...] = jnp.where(lane == 0, squares, jnp.where(lane == 1, dots, 0.0)).T[:8]


def forward_kernel(turned, part, onward):
    added = jnp.where(in_middle(part.shape), turned[...].astype(F32), 0.0)
    onward[...] = (part[...].astype(F32) + added).astype(BF16)


def gather_kernel(lane_count, group, cap, other_ref, own_ref, pos_ref, grad, hidden, *refs):
    payloads, (send_table, place_table) = refs[:lane_count], refs[lane_count:]
    rows = lane_count * group
    slots = lane_count * cap
    block, tokens = own_ref.shape[1], grad.shape[0]
    lane = lax.axis_index("lane")
    row_id = iota((rows, block), 0)
    lane_id = (row_id >> int(math.log2(group))) ^ lane
    place = row_id & (group - 1)
    entry = place & (2 * cap - 1)
    earlier = mask(iota((block, block), 0) < iota((block, block), 1))

    def select(dest, first):
        match = dest == lane_id
        rank = dot(mask(match), earlier)
        return match & (rank == (entry - first).astype(F32))

    own = select(own_ref[...], 0)
    other = select(other_ref[...], cap)
    lane_pick = mask((iota((rows, lane_count), 0) >> int(math.log2(group))) ^ lane == iota((rows, lane_count), 1))
    high, low = pos_ref[...] >> 7, pos_ref[...] & 127
    spread = dot(lane_pick, high.astype(F32).astype(BF16)) * 128.0 + dot(lane_pick, low.astype(F32).astype(BF16))
    chosen = (iota((rows, cap), 0) & (cap - 1)) == iota((rows, cap), 1)
    row_pos = jnp.sum(jnp.where(chosen, spread, 0.0), axis=1, keepdims=True)
    taken = row_pos == iota((rows, tokens), 1).astype(F32)
    taken_place = iota((rows, tokens), 0) & (group - 1)
    grad_folds = group // cap
    grad_width = grad.shape[1] // grad_folds
    grad_rows = jnp.zeros((rows, grad_width), F32)
    for i in range(grad_folds):
        here = (taken_place >= cap * i) & (taken_place < cap * (i + 1))
        grad_rows = grad_rows + dot(mask(taken & here), grad[:, i * grad_width : (i + 1) * grad_width])
    section = lax.axis_index("section")
    own_rows = pl.ds(pl.multiple_of(section * block, block), block)
    other_rows = pl.ds(pl.multiple_of((1 - section) * block, block), block)
    folds = group // (2 * cap)
    width = hidden.shape[1] // folds
    picked = jnp.zeros((rows, width), F32)
    for i in range(folds):
        here = (place >= 2 * cap * i) & (place < 2 * cap * (i + 1))
        cut = slice(i * width, (i + 1) * width)
        picked = picked + dot(mask(own & here), hidden[own_rows, cut]) + dot(mask(other & here), hidden[other_rows, cut])
    active = 0.5 * picked * (1.0 + lax.erf(picked * np.float32(math.sqrt(0.5))))

    for k in range(lane_count):
        cut = slice(k * group, (k + 1) * group)
        payloads[k][:, :width] = active[cut].astype(BF16)
        payloads[k][:, width:] = grad_rows[cut].astype(BF16)
    first = picker(slots, rows, group, cap, 0)
    send_table[...] = dot(first, mask(own)).astype(BF16)
    place_table[...] = dot(first, mask(taken)).astype(BF16)


def merge_kernel(lane_count, cap, *refs):
    got_refs, sent_refs = (refs[0],) + refs[lane_count : 2 * lane_count - 1], refs[:lane_count]
    weight, own, other, grad_rows = refs[2 * lane_count - 1 :]
    group = refs[0].shape[0]
    rows = lane_count * group
    slots = lane_count * cap
    grad_width = grad_rows.shape[1] // (group // cap)
    width = refs[0].shape[1] - grad_width
    got = jnp.concatenate([ref[...] for ref in got_refs], axis=0)
    sent = jnp.concatenate([ref[...] for ref in sent_refs], axis=0)

    def unfold(table, firsts, step, cols):
        pieces = []
        for i in range(0, group, step):
            picks = jnp.concatenate([picker(slots, rows, group, cap, first + i) for first in firsts], axis=0)
            pieces.append(dot(picks, table[:, cols]))
        return jnp.concatenate(pieces, axis=1).astype(BF16)

    merged = slice(0, width)
    got_rows, sent_rows = unfold(got, (0, cap), 2 * cap, merged), unfold(sent, (0, cap), 2 * cap, merged)
    picked = jnp.concatenate([got_rows[:slots], sent_rows[:slots], got_rows[slots:], sent_rows[slots:]], axis=0)
    grad_rows[:slots] = unfold(sent, (0,), cap, slice(width, width + grad_width))
    grad_rows[slots:] = unfold(got, (0,), cap, slice(width, width + grad_width))
    cols = weight.shape[1]
    step = min(512, cols)
    for c in range(0, cols, step):
        total = dot(picked, weight[:, c : c + step])
        own[:, c : c + step] = total[: 2 * slots]
        other[:, c : c + step] = total[2 * slots :].astype(BF16)


def slot_kernel(
    tp_count, own, other, bias, gain, weight, grad_rows, text_sums, text_part, first_arrived, rows, text_total, *messages
):
    arrived = first_arrived[...].astype(F32)
    if tp_count == 4:
        arrived = jnp.where(in_middle(arrived.shape), arrived, 0.0)
    text_total[...] = text_part[...] + arrived
    slots2 = own.shape[0]
    slots = slots2 // 2
    placed = (own[...] + other[...].astype(F32) + bias[...]).astype(BF16)
    rows[...] = placed
    wide = placed.astype(F32)
    squares = jnp.sum(wide * wide, axis=1, keepdims=True)
    scaled = (wide * gain[...]).astype(BF16)
    cols = messages[0].shape[1] - 128
    dots = jnp.zeros_like(squares)
    for k in range(tp_count):
        span = peer_columns("tp", k, cols)
        part = dot(scaled, weight[:, span])
        dots = dots + jnp.sum(part * grad_rows[:, span].astype(F32), axis=1, keepdims=True)
        messages[k][:, :cols] = part[:slots].astype(BF16)
    lane = iota((slots2, 128), 1)
    columns = jnp.where(lane == 0, squares, jnp.where(lane == 1, dots, 0.0))
    padded = round_up(slots2, 128)
    if padded > slots2:
        columns = jnp.concatenate([columns, jnp.zeros((padded - slots2, 128), F32)], axis=0)
    turned = columns.T
    pieces = []
    for i in range(2):
        total = jnp.concatenate([text_sums[i : i + 1], turned[i : i + 1]], axis=1)
        high = total.astype(BF16).astype(F32)
        pieces += [high, total - high]
    line = jnp.concatenate(pieces, axis=1)
    message = jnp.zeros((slots, 128), F32)
    sublane = iota((slots, 128), 0)
    for i in range(line.shape[1] // 128):
        message = jnp.where(sublane == i, line[:, i * 128 : (i + 1) * 128], message)
    for k in range(tp_count):
        messages[k][:, cols:] = message.astype(BF16)


def grad_kernel(grad, grad_rows, weight, gain, text, rows, place_table, out, stream):
    slots = grad_rows.shape[0] // 2
    joined = jnp.concatenate([grad[...], grad_rows[slots:]], axis=0)
    taken = dot_dims(place_table[...], jnp.ones((slots, 128), BF16), 0, 0)[:, 0:1] > 0.0
    step = min(512, weight.shape[0])
    for c in range(0, weight.shape[0], step):
        cut = slice(c, c + step)
        out[:, cut] = gain[:, cut] * dot_dims(joined, weight[cut, :], 1, 1)
        placed = dot_dims(place_table[...], rows[:slots, cut], 0, 0)
        stream[:, cut] = jnp.where(taken, placed, text[:, cut].astype(F32)).astype(BF16)


def final_kernel(tp_count, arrived_count, features, rows, scaled_grad, stream, place_table, send_table, *refs):
    messages, parts = refs[:tp_count], refs[tp_count : tp_count + arrived_count]
    key_value, embed_grad, image_grad, kv_buffer, embed_buffer, image_buffer, sem = refs[tp_count + arrived_count :]
    slots2 = rows.shape[0]
    slots = slots2 // 2
    tokens, cols = kv_buffer.shape
    total = messages[0][...].astype(F32)
    for message in messages[1:]:
        total = total + message[...].astype(F32)
    span = tokens + round_up(slots2, 128)
    line = jnp.concatenate([total[i : i + 1, cols:] for i in range(4 * span // 128)], axis=1)
    squares = line[:, :span] + line[:, span : 2 * span]
    dots = line[:, 2 * span : 3 * span] + line[:, 3 * span :]
    inv = lax.rsqrt(squares / features + EPSILON)
    slope = inv * inv * inv * dots / features
    sublane = iota((128, span), 0)
    turned = jnp.where(sublane == 0, inv, jnp.where(sublane == 1, slope, 0.0)).T
    slot_inv, slot_slope = turned[tokens : tokens + slots2, 0:1], turned[tokens : tokens + slots2, 1:2]
    table = place_table[...].astype(F32)
    taken = jnp.sum(table, axis=0, keepdims=True) > 0.0
    token_inv = jnp.where(taken, jnp.sum(table * slot_inv[:slots], axis=0, keepdims=True), inv[:, :tokens])
    token_slope = jnp.where(taken, jnp.sum(table * slot_slope[:slots], axis=0, keepdims=True), slope[:, :tokens])
    sublane = iota((128, tokens), 0)
    lines = jnp.where(sublane == 0, token_inv, jnp.where(sublane == 1, token_slope, 0.0))
    turned = jnp.where(sublane == 2, taken.astype(F32), lines).T
    inv_col, slope_col, taken_col = turned[:, 0:1], turned[:, 1:2], turned[:, 2:3] > 0.0

    copies = []

    def send(source, target):
        copy = pltpu.make_async_copy(source, target, sem.at[len(copies)])
        copy.start()
        copies.append(copy)

    step = max(128, stream.shape[1] // PIECES)
    for c in range(0, stream.shape[1], step):
        cut = slice(c, c + step)
        embed_buffer[:, cut] = (inv_col * scaled_grad[:tokens, cut] - stream[:, cut].astype(F32) * slope_col).astype(BF16)
        send(embed_buffer.at[:, cut], embed_grad.at[:, cut])
        row_grad = slot_inv[slots:] * scaled_grad[tokens:, cut] - rows[slots:, cut].astype(F32) * slot_slope[slots:]
        image_buffer[:, cut] = dot_dims(send_table[...], row_grad.astype(BF16), 0, 0).astype(BF16)
        send(image_buffer.at[:, cut], image_grad.at[:, cut])
    kv_rows = (total[:, :cols] * slot_inv[:slots]).astype(BF16)
    kv_total = parts[0][...]
    for part in parts[1:]:
        kv_total = kv_total + part[...].astype(F32)
    kv_buffer[...] = jnp.where(taken_col, dot_dims(place_table[...], kv_rows, 0, 0), kv_total * inv_col).astype(BF16)
    send(kv_buffer, key_value)
    for copy in copies:
        copy.wait()


def params(mib=16):
    return pltpu.CompilerParams(vmem_limit_bytes=mib * MIB)


def cost_of(flops):
    return pl.CostEstimate(flops=flops, bytes_accessed=1024, transcendentals=0)


COST = cost_of(1024)
CHUNKS = 4
PIECES = 1
MERGE_COST = cost_of(1024)
GRAD_COST = cost_of(1000000000)
TEXT_COST = cost_of(1024)
SLOT_COST = cost_of(1024)
GATHER_COST = cost_of(4000000000)


def shape(dims, dtype):
    return jax.ShapeDtypeStruct(dims, dtype)


def call(kernel, name, operands, in_specs, outs, out_specs=None, scratch=(), cost=COST):
    return pl.pallas_call(
        kernel,
        out_shape=outs,
        in_specs=in_specs,
        out_specs=out_specs or [VMEM] * len(outs),
        scratch_shapes=scratch,
        compiler_params=params(),
        cost_estimate=cost,
        name=name,
    )(*operands)


def in_hbm(array):
    return pltpu.with_memory_space_constraint(array, pltpu.HBM)


def swap(array, axis, k):
    return lax.ppermute(array, axis, [(i, i ^ k) for i in range(lax.axis_size(axis))])


def on_device(
    merge_hidden, merge_weight, merge_bias, row_dest, image_pos, text_embed, norm_gain, kv_weight, kv_grad
):
    lane_count, tp_count = lax.axis_size("lane"), lax.axis_size("tp")
    tokens, features = text_embed.shape
    kv_cols = kv_weight.shape[1]
    cols = kv_cols // tp_count
    cap = image_pos.shape[3]
    slots = lane_count * cap
    slots2 = 2 * slots
    group = max(16, 2 * cap)
    width = merge_hidden.shape[1] // (group // (2 * cap)) + kv_cols // (group // cap)
    block = row_dest.shape[0]
    gain = norm_gain.reshape(1, features)
    bias = merge_bias.reshape(1, features)
    own_dest = row_dest.reshape(1, block)
    positions = image_pos.reshape(lane_count, cap)

    first = 3 if tp_count == 4 else tp_count // 2
    first_part, scaled, text, own_dest, positions = call(
        lambda *refs: first_text_kernel(first, *refs),
        "first_text_kv",
        [in_hbm(array) for array in (text_embed, gain, kv_weight, own_dest, positions)],
        [ANY] * 5,
        [shape((tokens, cols), BF16), shape((tokens, features), BF16)]
        + [pltpu.VMEM(array.shape, array.dtype) for array in (text_embed, own_dest, positions)],
        scratch=[
            pltpu.VMEM((1, features), F32),
            pltpu.VMEM((features, cols), BF16),
            pltpu.SemaphoreType.DMA((2 * CHUNKS + 3,)),
        ],
    )
    if tp_count == 4:
        turned = swap(first_part, "tp", 1)
        sections = lax.axis_size("section")
        pairs = [
            (section * 4 + z, section * 4 + 3 - z if z in (1, 2) else (section + 1) % sections * 4 + z)
            for section in range(sections)
            for z in range(4)
        ]
        first_arrived = lax.ppermute(first_part, ("section", "tp"), pairs)
    else:
        first_arrived = swap(first_part, "tp", first)

    other_dest = swap(own_dest, "section", 1)
    *sent, send_table, place_table = call(
        lambda *refs: gather_kernel(lane_count, group, cap, *refs),
        "gather_rows",
        [other_dest, own_dest, positions, kv_grad, merge_hidden],
        [VMEM] * 5,
        [shape((group, width), BF16)] * lane_count
        + [shape((slots, block), BF16), shape((slots, tokens), BF16)],
        cost=GATHER_COST,
    )
    send_table, kv_weight, merge_weight = lax.optimization_barrier((send_table, kv_weight, merge_weight))
    got = [swap(sent[k], "lane", k) for k in range(1, lane_count)]

    steps = [k for k in range(tp_count - 1, 0, -1) if k != first] + [0]
    *parts, text_own, text_sums = call(
        lambda *refs: text_kernel(first, steps, *refs),
        "text_kv",
        [scaled, kv_weight, kv_grad, text, first_part],
        [VMEM] * 5,
        [shape((tokens, cols), BF16)] * (tp_count - 2) + [shape((tokens, cols), F32), shape((8, tokens), F32)],
        cost=TEXT_COST,
    )
    if tp_count == 4:
        (parts[0],) = call(forward_kernel, "forward", [turned, parts[0]], [VMEM] * 2, [shape((tokens, cols), BF16)])
        parts = list(lax.optimization_barrier(tuple(parts)))
    arrived = [swap(part, "tp", k) for part, k in zip(parts, steps)]

    own, other, grad_rows = call(
        lambda *refs: merge_kernel(lane_count, cap, *refs),
        "merge_rows",
        [*sent, *got, merge_weight],
        [VMEM] * (2 * lane_count),
        [shape((slots2, features), F32), shape((slots2, features), BF16), shape((slots2, kv_cols), BF16)],
        cost=MERGE_COST,
    )
    other = swap(other, "section", 1)

    placed, text_total, *messages = call(
        lambda *refs: slot_kernel(tp_count, *refs),
        "slot_kv",
        [own, other, bias, gain, kv_weight, grad_rows, text_sums, text_own, first_arrived],
        [VMEM] * 9,
        [shape((slots2, features), BF16), shape((tokens, cols), F32)]
        + [shape((slots, cols + 128), BF16)] * tp_count,
        cost=SLOT_COST,
    )
    messages = [swap(messages[k], "tp", k) for k in range(tp_count - 1, 0, -1)] + [messages[0]]

    scaled_grad, stream = call(
        grad_kernel,
        "normed_grad",
        [kv_grad, grad_rows, kv_weight, gain, text, placed, place_table],
        [VMEM] * 7,
        [shape((tokens + slots, features), F32), shape((tokens, features), BF16)],
        cost=GRAD_COST,
    )

    key_value, embed_grad, image_grad = call(
        lambda *refs: final_kernel(tp_count, tp_count - 1, features * tp_count, *refs),
        "outputs",
        [placed, scaled_grad, stream, place_table, send_table, *messages, text_total, *arrived],
        [VMEM] * (4 + 2 * tp_count),
        [shape((tokens, cols), BF16), shape((tokens, features), BF16), shape((block, features), BF16)],
        out_specs=[ANY] * 3,
        scratch=[
            pltpu.VMEM((tokens, cols), BF16),
            pltpu.VMEM((tokens, features), BF16),
            pltpu.VMEM((block, features), BF16),
            pltpu.SemaphoreType.DMA((2 * PIECES + 1,)),
        ],
    )
    return (key_value, embed_grad, image_grad)


def solution(mesh):
    in_specs = (
        P("lane", "section"),
        P("section", "tp"),
        P("tp"),
        P(("lane", "section")),
        P("lane", "section", None, None),
        P(("lane", "section"), "tp"),
        P("tp"),
        P("tp", None),
        P(("lane", "section"), None),
    )
    out_specs = (
        P(("lane", "section"), "tp"),
        P(("lane", "section"), "tp"),
        P(("lane", "section"), "tp"),
    )
    return jax.shard_map(
        on_device, mesh=mesh, in_specs=in_specs, out_specs=out_specs, check_vma=False
    )
```

```python
import math

import jax
import jax.numpy as jnp
import numpy as np
from jax import lax
from jax.experimental import pallas as pl
from jax.experimental.pallas import tpu as pltpu
from jax.sharding import PartitionSpec as P

EPSILON = 1e-06
F32 = jnp.float32
BF16 = jnp.bfloat16
MIB = 1 << 20
VMEM = pl.BlockSpec(memory_space=pltpu.VMEM)
ANY = pl.BlockSpec(memory_space=pl.ANY)


def round_up(value, step):
    return -(-value // step) * step


def dot(a, b):
    return jnp.dot(a, b, preferred_element_type=F32)


def dot_dims(a, b, dim_a, dim_b):
    return lax.dot_general(a, b, (((dim_a,), (dim_b,)), ((), ())), preferred_element_type=F32)


def iota(shape, dim):
    return lax.broadcasted_iota(jnp.int32, shape, dim)


def one_hot(column, width):
    return (column == iota((column.shape[0], width), 1)).astype(F32).astype(BF16)


def peer_columns(axis, k, cols):
    return pl.ds(pl.multiple_of((lax.axis_index(axis) ^ k) * cols, cols), cols)


def in_middle(dims):
    place = jnp.full(dims, lax.axis_index("tp"), jnp.int32)
    return (place == 1) | (place == 2)


def picker(slots, rows, group, cap, first):
    row = iota((slots, rows), 1)
    place = (row & (group - 1)) - first
    slot = (row >> int(math.log2(group))) * cap + place
    return ((slot == iota((slots, rows), 0)) & (place >= 0) & (place < cap)).astype(F32).astype(BF16)


def mask(match):
    return match.astype(F32).astype(BF16)


def first_text_kernel(step, text_hbm, gain_hbm, weight_hbm, dest_hbm, pos_hbm, part, scaled, text, dest, pos, gain, weight, sem):
    span = peer_columns("tp", step, part.shape[1])
    count = CHUNKS if text.shape[1] % 512 == 0 else 1
    size = text.shape[1] // count
    cuts = [slice(i * size, (i + 1) * size) for i in range(count)]
    copies = []
    for i, cut in enumerate(cuts):
        pair = (
            pltpu.make_async_copy(text_hbm.at[:, cut], text.at[:, cut], sem.at[2 * i + 1]),
            pltpu.make_async_copy(weight_hbm.at[cut, span], weight.at[cut], sem.at[2 * i + 2]),
        )
        for copy in pair:
            copy.start()
        copies.append(pair)
        if i == 0:
            gain_copy = pltpu.make_async_copy(gain_hbm, gain, sem.at[0])
            gain_copy.start()
    small = [pltpu.make_async_copy(*pair, sem.at[2 * count + 1 + i]) for i, pair in enumerate([(dest_hbm, dest), (pos_hbm, pos)])]
    for copy in small:
        copy.start()
    gain_copy.wait()
    total = jnp.zeros(part.shape, F32)
    for cut, pair in zip(cuts, copies):
        pair[0].wait()
        scaled[:, cut] = (text[:, cut].astype(F32) * gain[:, cut]).astype(BF16)
        pair[1].wait()
        total = total + dot(scaled[:, cut], weight[cut])
    part[...] = total.astype(BF16)
    for copy in small:
        copy.wait()


def text_kernel(first_step, steps, scaled, weight, grad, text, first_part, *refs):
    parts, sums = refs[:-1], refs[-1]
    cols = parts[0].shape[1]

    def row_dots(product, span):
        return jnp.sum(product * grad[:, span].astype(F32), axis=1, keepdims=True)

    dots = row_dots(first_part[...].astype(F32), peer_columns("tp", first_step, cols))
    for step, part in zip(steps, parts):
        span = peer_columns("tp", step, cols)
        product = dot(scaled[...], weight[:, span])
        part[...] = product.astype(part.dtype)
        dots = dots + row_dots(product, span)
    wide = text[...].astype(F32)
    squares = jnp.sum(wide * wide, axis=1, keepdims=True)
    lane = iota((text.shape[0], 128), 1)
    sums[...] = jnp.where(lane == 0, squares, jnp.where(lane == 1, dots, 0.0)).T[:8]


def forward_kernel(turned, part, onward):
    added = jnp.where(in_middle(part.shape), turned[...].astype(F32), 0.0)
    onward[...] = (part[...].astype(F32) + added).astype(BF16)


def gather_kernel(lane_count, group, cap, other_ref, own_ref, pos_ref, grad, hidden, *refs):
    payloads, (send_table, place_table) = refs[:lane_count], refs[lane_count:]
    rows = lane_count * group
    slots = lane_count * cap
    block, tokens = own_ref.shape[1], grad.shape[0]
    lane = lax.axis_index("lane")
    row_id = iota((rows, block), 0)
    lane_id = (row_id >> int(math.log2(group))) ^ lane
    place = row_id & (group - 1)
    entry = place & (2 * cap - 1)
    earlier = mask(iota((block, block), 0) < iota((block, block), 1))

    def select(dest, first):
        match = dest == lane_id
        rank = dot(mask(match), earlier)
        return match & (rank == (entry - first).astype(F32))

    own = select(own_ref[...], 0)
    other = select(other_ref[...], cap)
    lane_pick = mask((iota((rows, lane_count), 0) >> int(math.log2(group))) ^ lane == iota((rows, lane_count), 1))
    high, low = pos_ref[...] >> 7, pos_ref[...] & 127
    spread = dot(lane_pick, high.astype(F32).astype(BF16)) * 128.0 + dot(lane_pick, low.astype(F32).astype(BF16))
    chosen = (iota((rows, cap), 0) & (cap - 1)) == iota((rows, cap), 1)
    row_pos = jnp.sum(jnp.where(chosen, spread, 0.0), axis=1, keepdims=True)
    taken = row_pos == iota((rows, tokens), 1).astype(F32)
    taken_place = iota((rows, tokens), 0) & (group - 1)
    grad_folds = group // cap
    grad_width = grad.shape[1] // grad_folds
    grad_rows = jnp.zeros((rows, grad_width), F32)
    for i in range(grad_folds):
        here = (taken_place >= cap * i) & (taken_place < cap * (i + 1))
        grad_rows = grad_rows + dot(mask(taken & here), grad[:, i * grad_width : (i + 1) * grad_width])
    section = lax.axis_index("section")
    own_rows = pl.ds(pl.multiple_of(section * block, block), block)
    other_rows = pl.ds(pl.multiple_of((1 - section) * block, block), block)
    folds = group // (2 * cap)
    width = hidden.shape[1] // folds
    picked = jnp.zeros((rows, width), F32)
    for i in range(folds):
        here = (place >= 2 * cap * i) & (place < 2 * cap * (i + 1))
        cut = slice(i * width, (i + 1) * width)
        picked = picked + dot(mask(own & here), hidden[own_rows, cut]) + dot(mask(other & here), hidden[other_rows, cut])
    active = 0.5 * picked * (1.0 + lax.erf(picked * np.float32(math.sqrt(0.5))))

    for k in range(lane_count):
        cut = slice(k * group, (k + 1) * group)
        payloads[k][:, :width] = active[cut].astype(BF16)
        payloads[k][:, width:] = grad_rows[cut].astype(BF16)
    first = picker(slots, rows, group, cap, 0)
    send_table[...] = dot(first, mask(own)).astype(BF16)
    place_table[...] = dot(first, mask(taken)).astype(BF16)


def merge_kernel(lane_count, cap, *refs):
    got_refs, sent_refs = (refs[0],) + refs[lane_count : 2 * lane_count - 1], refs[:lane_count]
    weight, own, other, grad_rows = refs[2 * lane_count - 1 :]
    group = refs[0].shape[0]
    rows = lane_count * group
    slots = lane_count * cap
    grad_width = grad_rows.shape[1] // (group // cap)
    width = refs[0].shape[1] - grad_width
    got = jnp.concatenate([ref[...] for ref in got_refs], axis=0)
    sent = jnp.concatenate([ref[...] for ref in sent_refs], axis=0)

    def unfold(table, firsts, step, cols):
        pieces = []
        for i in range(0, group, step):
            picks = jnp.concatenate([picker(slots, rows, group, cap, first + i) for first in firsts], axis=0)
            pieces.append(dot(picks, table[:, cols]))
        return jnp.concatenate(pieces, axis=1).astype(BF16)

    merged = slice(0, width)
    got_rows, sent_rows = unfold(got, (0, cap), 2 * cap, merged), unfold(sent, (0, cap), 2 * cap, merged)
    picked = jnp.concatenate([got_rows[:slots], sent_rows[:slots], got_rows[slots:], sent_rows[slots:]], axis=0)
    grad_rows[:slots] = unfold(sent, (0,), cap, slice(width, width + grad_width))
    grad_rows[slots:] = unfold(got, (0,), cap, slice(width, width + grad_width))
    cols = weight.shape[1]
    step = min(512, cols)
    for c in range(0, cols, step):
        total = dot(picked, weight[:, c : c + step])
        own[:, c : c + step] = total[: 2 * slots]
        other[:, c : c + step] = total[2 * slots :].astype(BF16)


def slot_kernel(
    tp_count, own, other, bias, gain, weight, grad_rows, text_sums, text_part, first_arrived, rows, text_total, *messages
):
    arrived = first_arrived[...].astype(F32)
    if tp_count == 4:
        arrived = jnp.where(in_middle(arrived.shape), arrived, 0.0)
    text_total[...] = text_part[...] + arrived
    slots2 = own.shape[0]
    slots = slots2 // 2
    placed = (own[...] + other[...].astype(F32) + bias[...]).astype(BF16)
    rows[...] = placed
    wide = placed.astype(F32)
    squares = jnp.sum(wide * wide, axis=1, keepdims=True)
    scaled = (wide * gain[...]).astype(BF16)
    cols = messages[0].shape[1] - 128
    dots = jnp.zeros_like(squares)
    for k in range(tp_count):
        span = peer_columns("tp", k, cols)
        part = dot(scaled, weight[:, span])
        dots = dots + jnp.sum(part * grad_rows[:, span].astype(F32), axis=1, keepdims=True)
        messages[k][:, :cols] = part[:slots].astype(BF16)
    lane = iota((slots2, 128), 1)
    columns = jnp.where(lane == 0, squares, jnp.where(lane == 1, dots, 0.0))
    padded = round_up(slots2, 128)
    if padded > slots2:
        columns = jnp.concatenate([columns, jnp.zeros((padded - slots2, 128), F32)], axis=0)
    turned = columns.T
    pieces = []
    for i in range(2):
        total = jnp.concatenate([text_sums[i : i + 1], turned[i : i + 1]], axis=1)
        high = total.astype(BF16).astype(F32)
        pieces += [high, total - high]
    line = jnp.concatenate(pieces, axis=1)
    message = jnp.zeros((slots, 128), F32)
    sublane = iota((slots, 128), 0)
    for i in range(line.shape[1] // 128):
        message = jnp.where(sublane == i, line[:, i * 128 : (i + 1) * 128], message)
    for k in range(tp_count):
        messages[k][:, cols:] = message.astype(BF16)


def grad_kernel(grad, grad_rows, weight, gain, text, rows, place_table, out, stream):
    slots = grad_rows.shape[0] // 2
    joined = jnp.concatenate([grad[...], grad_rows[slots:]], axis=0)
    taken = dot_dims(place_table[...], jnp.ones((slots, 128), BF16), 0, 0)[:, 0:1] > 0.0
    step = min(512, weight.shape[0])
    for c in range(0, weight.shape[0], step):
        cut = slice(c, c + step)
        out[:, cut] = gain[:, cut] * dot_dims(joined, weight[cut, :], 1, 1)
        placed = dot_dims(place_table[...], rows[:slots, cut], 0, 0)
        stream[:, cut] = jnp.where(taken, placed, text[:, cut].astype(F32)).astype(BF16)


def final_kernel(tp_count, arrived_count, features, rows, scaled_grad, stream, place_table, send_table, *refs):
    messages, parts = refs[:tp_count], refs[tp_count : tp_count + arrived_count]
    key_value, embed_grad, image_grad, kv_buffer, embed_buffer, image_buffer, sem = refs[tp_count + arrived_count :]
    slots2 = rows.shape[0]
    slots = slots2 // 2
    tokens, cols = kv_buffer.shape
    total = messages[0][...].astype(F32)
    for message in messages[1:]:
        total = total + message[...].astype(F32)
    span = tokens + round_up(slots2, 128)
    line = jnp.concatenate([total[i : i + 1, cols:] for i in range(4 * span // 128)], axis=1)
    squares = line[:, :span] + line[:, span : 2 * span]
    dots = line[:, 2 * span : 3 * span] + line[:, 3 * span :]
    inv = lax.rsqrt(squares / features + EPSILON)
    slope = inv * inv * inv * dots / features
    sublane = iota((128, span), 0)
    turned = jnp.where(sublane == 0, inv, jnp.where(sublane == 1, slope, 0.0)).T
    slot_inv, slot_slope = turned[tokens : tokens + slots2, 0:1], turned[tokens : tokens + slots2, 1:2]
    table = place_table[...].astype(F32)
    taken = jnp.sum(table, axis=0, keepdims=True) > 0.0
    token_inv = jnp.where(taken, jnp.sum(table * slot_inv[:slots], axis=0, keepdims=True), inv[:, :tokens])
    token_slope = jnp.where(taken, jnp.sum(table * slot_slope[:slots], axis=0, keepdims=True), slope[:, :tokens])
    sublane = iota((128, tokens), 0)
    lines = jnp.where(sublane == 0, token_inv, jnp.where(sublane == 1, token_slope, 0.0))
    turned = jnp.where(sublane == 2, taken.astype(F32), lines).T
    inv_col, slope_col, taken_col = turned[:, 0:1], turned[:, 1:2], turned[:, 2:3] > 0.0

    copies = []

    def send(source, target):
        copy = pltpu.make_async_copy(source, target, sem.at[len(copies)])
        copy.start()
        copies.append(copy)

    step = max(128, stream.shape[1] // PIECES)
    for c in range(0, stream.shape[1], step):
        cut = slice(c, c + step)
        embed_buffer[:, cut] = (inv_col * scaled_grad[:tokens, cut] - stream[:, cut].astype(F32) * slope_col).astype(BF16)
        send(embed_buffer.at[:, cut], embed_grad.at[:, cut])
        row_grad = slot_inv[slots:] * scaled_grad[tokens:, cut] - rows[slots:, cut].astype(F32) * slot_slope[slots:]
        image_buffer[:, cut] = dot_dims(send_table[...], row_grad.astype(BF16), 0, 0).astype(BF16)
        send(image_buffer.at[:, cut], image_grad.at[:, cut])
    kv_rows = (total[:, :cols] * slot_inv[:slots]).astype(BF16)
    kv_total = parts[0][...]
    for part in parts[1:]:
        kv_total = kv_total + part[...].astype(F32)
    kv_buffer[...] = jnp.where(taken_col, dot_dims(place_table[...], kv_rows, 0, 0), kv_total * inv_col).astype(BF16)
    send(kv_buffer, key_value)
    for copy in copies:
        copy.wait()


def params(mib=16):
    return pltpu.CompilerParams(vmem_limit_bytes=mib * MIB)


def cost_of(flops):
    return pl.CostEstimate(flops=flops, bytes_accessed=1024, transcendentals=0)


COST = cost_of(1024)
CHUNKS = 4
PIECES = 1
MERGE_COST = cost_of(1024)
GRAD_COST = cost_of(1000000000)
TEXT_COST = cost_of(1024)
SLOT_COST = cost_of(1024)
GATHER_COST = cost_of(4000000000)


def shape(dims, dtype):
    return jax.ShapeDtypeStruct(dims, dtype)


def call(kernel, name, operands, in_specs, outs, out_specs=None, scratch=(), cost=COST):
    return pl.pallas_call(
        kernel,
        out_shape=outs,
        in_specs=in_specs,
        out_specs=out_specs or [VMEM] * len(outs),
        scratch_shapes=scratch,
        compiler_params=params(),
        cost_estimate=cost,
        name=name,
    )(*operands)


def in_hbm(array):
    return pltpu.with_memory_space_constraint(array, pltpu.HBM)


def swap(array, axis, k):
    return lax.ppermute(array, axis, [(i, i ^ k) for i in range(lax.axis_size(axis))])


def on_device(
    merge_hidden, merge_weight, merge_bias, row_dest, image_pos, text_embed, norm_gain, kv_weight, kv_grad
):
    lane_count, tp_count = lax.axis_size("lane"), lax.axis_size("tp")
    tokens, features = text_embed.shape
    kv_cols = kv_weight.shape[1]
    cols = kv_cols // tp_count
    cap = image_pos.shape[3]
    slots = lane_count * cap
    slots2 = 2 * slots
    group = max(16, 2 * cap)
    width = merge_hidden.shape[1] // (group // (2 * cap)) + kv_cols // (group // cap)
    block = row_dest.shape[0]
    gain = norm_gain.reshape(1, features)
    bias = merge_bias.reshape(1, features)
    own_dest = row_dest.reshape(1, block)
    positions = image_pos.reshape(lane_count, cap)

    first = 3 if tp_count == 4 else tp_count // 2
    first_part, scaled, text, own_dest, positions = call(
        lambda *refs: first_text_kernel(first, *refs),
        "first_text_kv",
        [in_hbm(array) for array in (text_embed, gain, kv_weight, own_dest, positions)],
        [ANY] * 5,
        [shape((tokens, cols), BF16), shape((tokens, features), BF16)]
        + [pltpu.VMEM(array.shape, array.dtype) for array in (text_embed, own_dest, positions)],
        scratch=[
            pltpu.VMEM((1, features), F32),
            pltpu.VMEM((features, cols), BF16),
            pltpu.SemaphoreType.DMA((2 * CHUNKS + 3,)),
        ],
    )
    if tp_count == 4:
        turned = swap(first_part, "tp", 1)
        sections = lax.axis_size("section")
        pairs = [
            (section * 4 + z, section * 4 + 3 - z if z in (1, 2) else (section + 1) % sections * 4 + z)
            for section in range(sections)
            for z in range(4)
        ]
        first_arrived = lax.ppermute(first_part, ("section", "tp"), pairs)
    else:
        first_arrived = swap(first_part, "tp", first)

    other_dest = swap(own_dest, "section", 1)
    *sent, send_table, place_table = call(
        lambda *refs: gather_kernel(lane_count, group, cap, *refs),
        "gather_rows",
        [other_dest, own_dest, positions, kv_grad, merge_hidden],
        [VMEM] * 5,
        [shape((group, width), BF16)] * lane_count
        + [shape((slots, block), BF16), shape((slots, tokens), BF16)],
        cost=GATHER_COST,
    )
    send_table, kv_weight, merge_weight = lax.optimization_barrier((send_table, kv_weight, merge_weight))
    got = [swap(sent[k], "lane", k) for k in range(1, lane_count)]

    steps = [k for k in range(tp_count - 1, 0, -1) if k != first] + [0]
    *parts, text_own, text_sums = call(
        lambda *refs: text_kernel(first, steps, *refs),
        "text_kv",
        [scaled, kv_weight, kv_grad, text, first_part],
        [VMEM] * 5,
        [shape((tokens, cols), BF16)] * (tp_count - 2) + [shape((tokens, cols), F32), shape((8, tokens), F32)],
        cost=TEXT_COST,
    )
    if tp_count == 4:
        (parts[0],) = call(forward_kernel, "forward", [turned, parts[0]], [VMEM] * 2, [shape((tokens, cols), BF16)])
        parts = list(lax.optimization_barrier(tuple(parts)))
    arrived = [swap(part, "tp", k) for part, k in zip(parts, steps)]

    own, other, grad_rows = call(
        lambda *refs: merge_kernel(lane_count, cap, *refs),
        "merge_rows",
        [*sent, *got, merge_weight],
        [VMEM] * (2 * lane_count),
        [shape((slots2, features), F32), shape((slots2, features), BF16), shape((slots2, kv_cols), BF16)],
        cost=MERGE_COST,
    )
    other = swap(other, "section", 1)

    placed, text_total, *messages = call(
        lambda *refs: slot_kernel(tp_count, *refs),
        "slot_kv",
        [own, other, bias, gain, kv_weight, grad_rows, text_sums, text_own, first_arrived],
        [VMEM] * 9,
        [shape((slots2, features), BF16), shape((tokens, cols), F32)]
        + [shape((slots, cols + 128), BF16)] * tp_count,
        cost=SLOT_COST,
    )
    farthest_first = [tp_count - 1] + list(range(1, tp_count - 1))
    messages = [swap(messages[k], "tp", k) for k in farthest_first] + [messages[0]]

    scaled_grad, stream = call(
        grad_kernel,
        "normed_grad",
        [kv_grad, grad_rows, kv_weight, gain, text, placed, place_table],
        [VMEM] * 7,
        [shape((tokens + slots, features), F32), shape((tokens, features), BF16)],
        cost=GRAD_COST,
    )

    key_value, embed_grad, image_grad = call(
        lambda *refs: final_kernel(tp_count, tp_count - 1, features * tp_count, *refs),
        "outputs",
        [placed, scaled_grad, stream, place_table, send_table, *messages, text_total, *arrived],
        [VMEM] * (4 + 2 * tp_count),
        [shape((tokens, cols), BF16), shape((tokens, features), BF16), shape((block, features), BF16)],
        out_specs=[ANY] * 3,
        scratch=[
            pltpu.VMEM((tokens, cols), BF16),
            pltpu.VMEM((tokens, features), BF16),
            pltpu.VMEM((block, features), BF16),
            pltpu.SemaphoreType.DMA((2 * PIECES + 1,)),
        ],
    )
    return (key_value, embed_grad, image_grad)


def solution(mesh):
    in_specs = (
        P("lane", "section"),
        P("section", "tp"),
        P("tp"),
        P(("lane", "section")),
        P("lane", "section", None, None),
        P(("lane", "section"), "tp"),
        P("tp"),
        P("tp", None),
        P(("lane", "section"), None),
    )
    out_specs = (
        P(("lane", "section"), "tp"),
        P(("lane", "section"), "tp"),
        P(("lane", "section"), "tp"),
    )
    return jax.shard_map(
        on_device, mesh=mesh, in_specs=in_specs, out_specs=out_specs, check_vma=False
    )
```

```python
import math

import jax
import jax.numpy as jnp
import numpy as np
from jax import lax
from jax.experimental import pallas as pl
from jax.experimental.pallas import tpu as pltpu
from jax.sharding import PartitionSpec as P

EPSILON = 1e-06
F32 = jnp.float32
BF16 = jnp.bfloat16
MIB = 1 << 20
VMEM = pl.BlockSpec(memory_space=pltpu.VMEM)
ANY = pl.BlockSpec(memory_space=pl.ANY)


def round_up(value, step):
    return -(-value // step) * step


def dot(a, b):
    return jnp.dot(a, b, preferred_element_type=F32)


def dot_dims(a, b, dim_a, dim_b):
    return lax.dot_general(a, b, (((dim_a,), (dim_b,)), ((), ())), preferred_element_type=F32)


def iota(shape, dim):
    return lax.broadcasted_iota(jnp.int32, shape, dim)


def one_hot(column, width):
    return (column == iota((column.shape[0], width), 1)).astype(F32).astype(BF16)


def peer_columns(axis, k, cols):
    return pl.ds(pl.multiple_of((lax.axis_index(axis) ^ k) * cols, cols), cols)


def in_middle(dims):
    place = jnp.full(dims, lax.axis_index("tp"), jnp.int32)
    return (place == 1) | (place == 2)


def picker(slots, rows, group, cap, first):
    row = iota((slots, rows), 1)
    place = (row & (group - 1)) - first
    slot = (row >> int(math.log2(group))) * cap + place
    return ((slot == iota((slots, rows), 0)) & (place >= 0) & (place < cap)).astype(F32).astype(BF16)


def mask(match):
    return match.astype(F32).astype(BF16)


def first_text_kernel(step, text_hbm, gain_hbm, weight_hbm, dest_hbm, pos_hbm, part, scaled, text, dest, pos, gain, weight, sem):
    span = peer_columns("tp", step, part.shape[1])
    count = CHUNKS if text.shape[1] % 512 == 0 else 1
    size = text.shape[1] // count
    cuts = [slice(i * size, (i + 1) * size) for i in range(count)]
    copies = []
    for i, cut in enumerate(cuts):
        pair = (
            pltpu.make_async_copy(text_hbm.at[:, cut], text.at[:, cut], sem.at[2 * i + 1]),
            pltpu.make_async_copy(weight_hbm.at[cut, span], weight.at[cut], sem.at[2 * i + 2]),
        )
        for copy in pair[::-1]:
            copy.start()
        copies.append(pair)
        if i == 0:
            gain_copy = pltpu.make_async_copy(gain_hbm, gain, sem.at[0])
            gain_copy.start()
    small = [pltpu.make_async_copy(*pair, sem.at[2 * count + 1 + i]) for i, pair in enumerate([(dest_hbm, dest), (pos_hbm, pos)])]
    for copy in small:
        copy.start()
    gain_copy.wait()
    total = jnp.zeros(part.shape, F32)
    for cut, pair in zip(cuts, copies):
        pair[0].wait()
        scaled[:, cut] = (text[:, cut].astype(F32) * gain[:, cut]).astype(BF16)
        pair[1].wait()
        total = total + dot(scaled[:, cut], weight[cut])
    part[...] = total.astype(BF16)
    for copy in small:
        copy.wait()


def text_kernel(first_step, steps, scaled, weight, grad, text, first_part, *refs):
    parts, sums = refs[:-1], refs[-1]
    cols = parts[0].shape[1]

    def row_dots(product, span):
        return jnp.sum(product * grad[:, span].astype(F32), axis=1, keepdims=True)

    dots = row_dots(first_part[...].astype(F32), peer_columns("tp", first_step, cols))
    for step, part in zip(steps, parts):
        span = peer_columns("tp", step, cols)
        product = dot(scaled[...], weight[:, span])
        part[...] = product.astype(part.dtype)
        dots = dots + row_dots(product, span)
    wide = text[...].astype(F32)
    squares = jnp.sum(wide * wide, axis=1, keepdims=True)
    lane = iota((text.shape[0], 128), 1)
    sums[...] = jnp.where(lane == 0, squares, jnp.where(lane == 1, dots, 0.0)).T[:8]


def forward_kernel(turned, part, onward):
    added = jnp.where(in_middle(part.shape), turned[...].astype(F32), 0.0)
    onward[...] = (part[...].astype(F32) + added).astype(BF16)


def gather_kernel(lane_count, group, cap, other_ref, own_ref, pos_ref, grad, hidden, *refs):
    payloads, (send_table, place_table) = refs[:lane_count], refs[lane_count:]
    rows = lane_count * group
    slots = lane_count * cap
    block, tokens = own_ref.shape[1], grad.shape[0]
    lane = lax.axis_index("lane")
    row_id = iota((rows, block), 0)
    lane_id = (row_id >> int(math.log2(group))) ^ lane
    place = row_id & (group - 1)
    entry = place & (2 * cap - 1)
    earlier = mask(iota((block, block), 0) < iota((block, block), 1))

    def select(dest, first):
        match = dest == lane_id
        rank = dot(mask(match), earlier)
        return match & (rank == (entry - first).astype(F32))

    own = select(own_ref[...], 0)
    other = select(other_ref[...], cap)
    lane_pick = mask((iota((rows, lane_count), 0) >> int(math.log2(group))) ^ lane == iota((rows, lane_count), 1))
    high, low = pos_ref[...] >> 7, pos_ref[...] & 127
    spread = dot(lane_pick, high.astype(F32).astype(BF16)) * 128.0 + dot(lane_pick, low.astype(F32).astype(BF16))
    chosen = (iota((rows, cap), 0) & (cap - 1)) == iota((rows, cap), 1)
    row_pos = jnp.sum(jnp.where(chosen, spread, 0.0), axis=1, keepdims=True)
    taken = row_pos == iota((rows, tokens), 1).astype(F32)
    taken_place = iota((rows, tokens), 0) & (group - 1)
    grad_folds = group // cap
    grad_width = grad.shape[1] // grad_folds
    grad_rows = jnp.zeros((rows, grad_width), F32)
    for i in range(grad_folds):
        here = (taken_place >= cap * i) & (taken_place < cap * (i + 1))
        grad_rows = grad_rows + dot(mask(taken & here), grad[:, i * grad_width : (i + 1) * grad_width])
    section = lax.axis_index("section")
    own_rows = pl.ds(pl.multiple_of(section * block, block), block)
    other_rows = pl.ds(pl.multiple_of((1 - section) * block, block), block)
    folds = group // (2 * cap)
    width = hidden.shape[1] // folds
    picked = jnp.zeros((rows, width), F32)
    for i in range(folds):
        here = (place >= 2 * cap * i) & (place < 2 * cap * (i + 1))
        cut = slice(i * width, (i + 1) * width)
        picked = picked + dot(mask(own & here), hidden[own_rows, cut]) + dot(mask(other & here), hidden[other_rows, cut])
    active = 0.5 * picked * (1.0 + lax.erf(picked * np.float32(math.sqrt(0.5))))

    for k in range(lane_count):
        cut = slice(k * group, (k + 1) * group)
        payloads[k][:, :width] = active[cut].astype(BF16)
        payloads[k][:, width:] = grad_rows[cut].astype(BF16)
    first = picker(slots, rows, group, cap, 0)
    send_table[...] = dot(first, mask(own)).astype(BF16)
    place_table[...] = dot(first, mask(taken)).astype(BF16)


def merge_kernel(lane_count, cap, *refs):
    got_refs, sent_refs = (refs[0],) + refs[lane_count : 2 * lane_count - 1], refs[:lane_count]
    weight, own, other, grad_rows = refs[2 * lane_count - 1 :]
    group = refs[0].shape[0]
    rows = lane_count * group
    slots = lane_count * cap
    grad_width = grad_rows.shape[1] // (group // cap)
    width = refs[0].shape[1] - grad_width
    got = jnp.concatenate([ref[...] for ref in got_refs], axis=0)
    sent = jnp.concatenate([ref[...] for ref in sent_refs], axis=0)

    def unfold(table, firsts, step, cols):
        pieces = []
        for i in range(0, group, step):
            picks = jnp.concatenate([picker(slots, rows, group, cap, first + i) for first in firsts], axis=0)
            pieces.append(dot(picks, table[:, cols]))
        return jnp.concatenate(pieces, axis=1).astype(BF16)

    merged = slice(0, width)
    got_rows, sent_rows = unfold(got, (0, cap), 2 * cap, merged), unfold(sent, (0, cap), 2 * cap, merged)
    picked = jnp.concatenate([got_rows[:slots], sent_rows[:slots], got_rows[slots:], sent_rows[slots:]], axis=0)
    grad_rows[:slots] = unfold(sent, (0,), cap, slice(width, width + grad_width))
    grad_rows[slots:] = unfold(got, (0,), cap, slice(width, width + grad_width))
    cols = weight.shape[1]
    step = min(512, cols)
    for c in range(0, cols, step):
        total = dot(picked, weight[:, c : c + step])
        own[:, c : c + step] = total[: 2 * slots]
        other[:, c : c + step] = total[2 * slots :].astype(BF16)


def slot_kernel(
    tp_count, own, other, bias, gain, weight, grad_rows, text_sums, text_part, first_arrived, rows, text_total, *messages
):
    arrived = first_arrived[...].astype(F32)
    if tp_count == 4:
        arrived = jnp.where(in_middle(arrived.shape), arrived, 0.0)
    text_total[...] = text_part[...] + arrived
    slots2 = own.shape[0]
    slots = slots2 // 2
    placed = (own[...] + other[...].astype(F32) + bias[...]).astype(BF16)
    rows[...] = placed
    wide = placed.astype(F32)
    squares = jnp.sum(wide * wide, axis=1, keepdims=True)
    scaled = (wide * gain[...]).astype(BF16)
    cols = messages[0].shape[1] - 128
    dots = jnp.zeros_like(squares)
    for k in range(tp_count):
        span = peer_columns("tp", k, cols)
        part = dot(scaled, weight[:, span])
        dots = dots + jnp.sum(part * grad_rows[:, span].astype(F32), axis=1, keepdims=True)
        messages[k][:, :cols] = part[:slots].astype(BF16)
    lane = iota((slots2, 128), 1)
    columns = jnp.where(lane == 0, squares, jnp.where(lane == 1, dots, 0.0))
    padded = round_up(slots2, 128)
    if padded > slots2:
        columns = jnp.concatenate([columns, jnp.zeros((padded - slots2, 128), F32)], axis=0)
    turned = columns.T
    pieces = []
    for i in range(2):
        total = jnp.concatenate([text_sums[i : i + 1], turned[i : i + 1]], axis=1)
        high = total.astype(BF16).astype(F32)
        pieces += [high, total - high]
    line = jnp.concatenate(pieces, axis=1)
    message = jnp.zeros((slots, 128), F32)
    sublane = iota((slots, 128), 0)
    for i in range(line.shape[1] // 128):
        message = jnp.where(sublane == i, line[:, i * 128 : (i + 1) * 128], message)
    for k in range(tp_count):
        messages[k][:, cols:] = message.astype(BF16)


def grad_kernel(grad, grad_rows, weight, gain, text, rows, place_table, out, stream):
    slots = grad_rows.shape[0] // 2
    joined = jnp.concatenate([grad[...], grad_rows[slots:]], axis=0)
    taken = dot_dims(place_table[...], jnp.ones((slots, 128), BF16), 0, 0)[:, 0:1] > 0.0
    step = min(512, weight.shape[0])
    for c in range(0, weight.shape[0], step):
        cut = slice(c, c + step)
        out[:, cut] = gain[:, cut] * dot_dims(joined, weight[cut, :], 1, 1)
        placed = dot_dims(place_table[...], rows[:slots, cut], 0, 0)
        stream[:, cut] = jnp.where(taken, placed, text[:, cut].astype(F32)).astype(BF16)


def final_kernel(tp_count, arrived_count, features, rows, scaled_grad, stream, place_table, send_table, *refs):
    messages, parts = refs[:tp_count], refs[tp_count : tp_count + arrived_count]
    key_value, embed_grad, image_grad, kv_buffer, embed_buffer, image_buffer, sem = refs[tp_count + arrived_count :]
    slots2 = rows.shape[0]
    slots = slots2 // 2
    tokens, cols = kv_buffer.shape
    total = messages[0][...].astype(F32)
    for message in messages[1:]:
        total = total + message[...].astype(F32)
    span = tokens + round_up(slots2, 128)
    line = jnp.concatenate([total[i : i + 1, cols:] for i in range(4 * span // 128)], axis=1)
    squares = line[:, :span] + line[:, span : 2 * span]
    dots = line[:, 2 * span : 3 * span] + line[:, 3 * span :]
    inv = lax.rsqrt(squares / features + EPSILON)
    slope = inv * inv * inv * dots / features
    sublane = iota((128, span), 0)
    turned = jnp.where(sublane == 0, inv, jnp.where(sublane == 1, slope, 0.0)).T
    slot_inv, slot_slope = turned[tokens : tokens + slots2, 0:1], turned[tokens : tokens + slots2, 1:2]
    table = place_table[...].astype(F32)
    taken = jnp.sum(table, axis=0, keepdims=True) > 0.0
    token_inv = jnp.where(taken, jnp.sum(table * slot_inv[:slots], axis=0, keepdims=True), inv[:, :tokens])
    token_slope = jnp.where(taken, jnp.sum(table * slot_slope[:slots], axis=0, keepdims=True), slope[:, :tokens])
    sublane = iota((128, tokens), 0)
    lines = jnp.where(sublane == 0, token_inv, jnp.where(sublane == 1, token_slope, 0.0))
    turned = jnp.where(sublane == 2, taken.astype(F32), lines).T
    inv_col, slope_col, taken_col = turned[:, 0:1], turned[:, 1:2], turned[:, 2:3] > 0.0

    copies = []

    def send(source, target):
        copy = pltpu.make_async_copy(source, target, sem.at[len(copies)])
        copy.start()
        copies.append(copy)

    step = max(128, stream.shape[1] // PIECES)
    for c in range(0, stream.shape[1], step):
        cut = slice(c, c + step)
        embed_buffer[:, cut] = (inv_col * scaled_grad[:tokens, cut] - stream[:, cut].astype(F32) * slope_col).astype(BF16)
        send(embed_buffer.at[:, cut], embed_grad.at[:, cut])
        row_grad = slot_inv[slots:] * scaled_grad[tokens:, cut] - rows[slots:, cut].astype(F32) * slot_slope[slots:]
        image_buffer[:, cut] = dot_dims(send_table[...], row_grad.astype(BF16), 0, 0).astype(BF16)
        send(image_buffer.at[:, cut], image_grad.at[:, cut])
    kv_rows = (total[:, :cols] * slot_inv[:slots]).astype(BF16)
    kv_total = parts[0][...]
    for part in parts[1:]:
        kv_total = kv_total + part[...].astype(F32)
    kv_buffer[...] = jnp.where(taken_col, dot_dims(place_table[...], kv_rows, 0, 0), kv_total * inv_col).astype(BF16)
    send(kv_buffer, key_value)
    for copy in copies:
        copy.wait()


def params(mib=16):
    return pltpu.CompilerParams(vmem_limit_bytes=mib * MIB)


def cost_of(flops):
    return pl.CostEstimate(flops=flops, bytes_accessed=1024, transcendentals=0)


COST = cost_of(1024)
CHUNKS = 4
PIECES = 1
MERGE_COST = cost_of(1024)
GRAD_COST = cost_of(1000000000)
TEXT_COST = cost_of(1024)
SLOT_COST = cost_of(1024)
GATHER_COST = cost_of(4000000000)


def shape(dims, dtype):
    return jax.ShapeDtypeStruct(dims, dtype)


def call(kernel, name, operands, in_specs, outs, out_specs=None, scratch=(), cost=COST):
    return pl.pallas_call(
        kernel,
        out_shape=outs,
        in_specs=in_specs,
        out_specs=out_specs or [VMEM] * len(outs),
        scratch_shapes=scratch,
        compiler_params=params(),
        cost_estimate=cost,
        name=name,
    )(*operands)


def in_hbm(array):
    return pltpu.with_memory_space_constraint(array, pltpu.HBM)


def swap(array, axis, k):
    return lax.ppermute(array, axis, [(i, i ^ k) for i in range(lax.axis_size(axis))])


def on_device(
    merge_hidden, merge_weight, merge_bias, row_dest, image_pos, text_embed, norm_gain, kv_weight, kv_grad
):
    lane_count, tp_count = lax.axis_size("lane"), lax.axis_size("tp")
    tokens, features = text_embed.shape
    kv_cols = kv_weight.shape[1]
    cols = kv_cols // tp_count
    cap = image_pos.shape[3]
    slots = lane_count * cap
    slots2 = 2 * slots
    group = max(16, 2 * cap)
    width = merge_hidden.shape[1] // (group // (2 * cap)) + kv_cols // (group // cap)
    block = row_dest.shape[0]
    gain = norm_gain.reshape(1, features)
    bias = merge_bias.reshape(1, features)
    own_dest = row_dest.reshape(1, block)
    positions = image_pos.reshape(lane_count, cap)

    first = 3 if tp_count == 4 else tp_count // 2
    first_part, scaled, text, own_dest, positions = call(
        lambda *refs: first_text_kernel(first, *refs),
        "first_text_kv",
        [in_hbm(array) for array in (text_embed, gain, kv_weight, own_dest, positions)],
        [ANY] * 5,
        [shape((tokens, cols), BF16), shape((tokens, features), BF16)]
        + [pltpu.VMEM(array.shape, array.dtype) for array in (text_embed, own_dest, positions)],
        scratch=[
            pltpu.VMEM((1, features), F32),
            pltpu.VMEM((features, cols), BF16),
            pltpu.SemaphoreType.DMA((2 * CHUNKS + 3,)),
        ],
    )
    if tp_count == 4:
        turned = swap(first_part, "tp", 1)
        sections = lax.axis_size("section")
        pairs = [
            (section * 4 + z, section * 4 + 3 - z if z in (1, 2) else (section + 1) % sections * 4 + z)
            for section in range(sections)
            for z in range(4)
        ]
        first_arrived = lax.ppermute(first_part, ("section", "tp"), pairs)
    else:
        first_arrived = swap(first_part, "tp", first)

    other_dest = swap(own_dest, "section", 1)
    *sent, send_table, place_table = call(
        lambda *refs: gather_kernel(lane_count, group, cap, *refs),
        "gather_rows",
        [other_dest, own_dest, positions, kv_grad, merge_hidden],
        [VMEM] * 5,
        [shape((group, width), BF16)] * lane_count
        + [shape((slots, block), BF16), shape((slots, tokens), BF16)],
        cost=GATHER_COST,
    )
    send_table, kv_weight, merge_weight = lax.optimization_barrier((send_table, kv_weight, merge_weight))
    got = [swap(sent[k], "lane", k) for k in range(1, lane_count)]

    steps = [k for k in range(tp_count - 1, 0, -1) if k != first] + [0]
    *parts, text_own, text_sums = call(
        lambda *refs: text_kernel(first, steps, *refs),
        "text_kv",
        [scaled, kv_weight, kv_grad, text, first_part],
        [VMEM] * 5,
        [shape((tokens, cols), BF16)] * (tp_count - 2) + [shape((tokens, cols), F32), shape((8, tokens), F32)],
        cost=TEXT_COST,
    )
    if tp_count == 4:
        (parts[0],) = call(forward_kernel, "forward", [turned, parts[0]], [VMEM] * 2, [shape((tokens, cols), BF16)])
        parts = list(lax.optimization_barrier(tuple(parts)))
    arrived = [swap(part, "tp", k) for part, k in zip(parts, steps)]

    own, other, grad_rows = call(
        lambda *refs: merge_kernel(lane_count, cap, *refs),
        "merge_rows",
        [*sent, *got, merge_weight],
        [VMEM] * (2 * lane_count),
        [shape((slots2, features), F32), shape((slots2, features), BF16), shape((slots2, kv_cols), BF16)],
        cost=MERGE_COST,
    )
    other = swap(other, "section", 1)

    placed, text_total, *messages = call(
        lambda *refs: slot_kernel(tp_count, *refs),
        "slot_kv",
        [own, other, bias, gain, kv_weight, grad_rows, text_sums, text_own, first_arrived],
        [VMEM] * 9,
        [shape((slots2, features), BF16), shape((tokens, cols), F32)]
        + [shape((slots, cols + 128), BF16)] * tp_count,
        cost=SLOT_COST,
    )
    farthest_first = [tp_count - 1] + list(range(1, tp_count - 1))
    messages = [swap(messages[k], "tp", k) for k in farthest_first] + [messages[0]]

    scaled_grad, stream = call(
        grad_kernel,
        "normed_grad",
        [kv_grad, grad_rows, kv_weight, gain, text, placed, place_table],
        [VMEM] * 7,
        [shape((tokens + slots, features), F32), shape((tokens, features), BF16)],
        cost=GRAD_COST,
    )

    key_value, embed_grad, image_grad = call(
        lambda *refs: final_kernel(tp_count, tp_count - 1, features * tp_count, *refs),
        "outputs",
        [placed, scaled_grad, stream, place_table, send_table, *messages, text_total, *arrived],
        [VMEM] * (4 + 2 * tp_count),
        [shape((tokens, cols), BF16), shape((tokens, features), BF16), shape((block, features), BF16)],
        out_specs=[ANY] * 3,
        scratch=[
            pltpu.VMEM((tokens, cols), BF16),
            pltpu.VMEM((tokens, features), BF16),
            pltpu.VMEM((block, features), BF16),
            pltpu.SemaphoreType.DMA((2 * PIECES + 1,)),
        ],
    )
    return (key_value, embed_grad, image_grad)


def solution(mesh):
    in_specs = (
        P("lane", "section"),
        P("section", "tp"),
        P("tp"),
        P(("lane", "section")),
        P("lane", "section", None, None),
        P(("lane", "section"), "tp"),
        P("tp"),
        P("tp", None),
        P(("lane", "section"), None),
    )
    out_specs = (
        P(("lane", "section"), "tp"),
        P(("lane", "section"), "tp"),
        P(("lane", "section"), "tp"),
    )
    return jax.shard_map(
        on_device, mesh=mesh, in_specs=in_specs, out_specs=out_specs, check_vma=False
    )
```
